768 devices in a mesh: row: 48 (over z, y_lo), col: 4 (over y_hi, core), dep: 4 (over x).
Axes of the slice: x: 4, y: 8 (y_hi: 2, y_lo: 4; y = y_hi * 4 + y_lo), z: 12, core: 2. Of those that a mesh axis runs over, the one named last changes fastest.
Arguments:
- amp_old: bfloat16 [960, 2, 480], P('row', None, 'dep'), may hold values from -6 to 6
- ladder_int: bfloat16 [480, 480, 2, 480], P('row', 'col', None, 'dep'), may hold values from -0.5 to 0.5
- cycle_int: bfloat16 [60, 64, 480], replicated, may hold values from -0.03125 to 0.03125
- virt_irrep: int32 [480], replicated, may hold values from 0 to 7
- occ_energy: float32 [60], replicated, may hold values from -3 to -0.5
- virt_energy: float32 [480], replicated, may hold values from 0.5 to 3
Outputs:
- new_amps: bfloat16 [16, 60, 480, 480], P(('col', 'dep'), None, 'row')
- cycle_term: float32 [16, 480, 64], P(('col', 'dep'), 'row')
The draws below stay inside these ranges and needn't reach their ends.
All inputs are finite; a program needn't handle non-finite values.
Results may differ from the reference program's by a relative error of at most 0.015.
Values may be sent and summed in bfloat16 or wider, within the bound.
A program may use at most 32 MiB of HBM per device.

```python
import jax
import jax.numpy as jnp
from jax import lax

O = 60
V = 480
CW = 2
RC = 64
IW = 16
NPAIR = 960
N_DEP = 4


def with_ends(drawn, rng, low, high):
    spot = [jax.random.randint(jax.random.fold_in(rng, axis), (), 0, length) for axis, length in enumerate(drawn.shape)]
    longest = drawn.shape.index(max(drawn.shape))
    next_to = spot[:longest] + [(spot[longest] + 1) % drawn.shape[longest]] + spot[longest + 1:]
    return drawn.at[tuple(spot)].set(low).at[tuple(next_to)].set(high)


def levels(own_key, dims, pieces, low, top_value):
    def one(dim, shards_of):
        steps = jax.random.uniform(jax.random.fold_in(jax.random.fold_in(own_key, 6), dim), (shards_of,), jnp.float32, low / len(pieces), top_value / len(pieces))
        return jnp.repeat(jnp.exp(steps), dims[dim] // shards_of).reshape((-1,) + (1,) * (len(dims) - dim - 1))

    level = one(*pieces[0])
    for cut in pieces[1:]:
        level = level * one(*cut)
    return level


def normal_values(rng, extent, width, reach, shards=(), kind=jnp.bfloat16):
    factor_of = levels(rng, extent, shards, -0.22, 0.18) if shards else 1.0
    values = jax.random.normal(rng, extent, jnp.float32) * width * factor_of
    return jnp.minimum(jnp.maximum(values, -reach), reach).astype(kind)


def setup_inputs(seed: int = 0) -> dict:
    keys = jax.random.split(jax.random.key(seed), 7)
    return {
        "amp_old": normal_values(keys[0], (NPAIR, CW, V), 1.0, 6.0, ((0, 48), (2, 4))),
        "ladder_int": normal_values(keys[1], (V, V, CW, V), (CW * V // 8) ** -0.5, 0.5, ((0, 48), (1, 4), (3, 4))),
        "cycle_int": normal_values(keys[2], (O, RC, V), (O * V) ** -0.5, 0.03125),
        "virt_irrep": with_ends(jax.random.randint(keys[3], (V,), 0, 8), jax.random.fold_in(keys[3], 1), 0, 7).astype(jnp.int32),
        "occ_energy": jnp.clip(jax.random.uniform(keys[4], (O,), jnp.float32, -3.0, -0.5), -3.0, -0.5),
        "virt_energy": jnp.clip(jax.random.uniform(keys[5], (V,), jnp.float32, 0.5, 3.0), 0.5, 3.0),
    }


def reference(amp_old, ladder_int, cycle_int, virt_irrep, occ_energy, virt_energy):
    labels = virt_irrep.astype(jnp.int32)
    depth = V // N_DEP
    amp_blocks = amp_old.reshape(NPAIR, CW, N_DEP, depth)
    pair_occ = jnp.repeat(occ_energy[:IW], O) + jnp.tile(occ_energy, IW)

    def ladder_row(a_index):
        sym = jnp.bitwise_xor(jnp.bitwise_xor(labels[a_index], labels[:, None, None]),
                              jnp.bitwise_xor(labels[None, :CW, None], labels[None, None, :])) == 0
        masked = jnp.where(sym, ladder_int[a_index], jnp.zeros((), jnp.bfloat16)).astype(jnp.bfloat16)
        masked = masked.reshape(V, CW, N_DEP, depth)
        total = jnp.zeros((NPAIR, V), jnp.float32)
        for block in range(N_DEP):
            left = amp_blocks[:, :, block, :].reshape(NPAIR, CW * depth)
            right = masked[:, :, block, :].reshape(V, CW * depth)
            piece = lax.dot_general(left, right, (((1,), (1,)), ((), ())), preferred_element_type=jnp.float32)
            piece = lax.optimization_barrier(piece.astype(jnp.bfloat16))
            total = total + piece.astype(jnp.float32)
        denom = virt_energy[a_index] + virt_energy[None, :] - pair_occ[:, None]
        return (total / denom).astype(jnp.bfloat16)

    rows = lax.map(ladder_row, jnp.arange(V, dtype=jnp.int32))
    new_amps = jnp.transpose(rows.reshape(V, IW, O, V), (1, 2, 0, 3))
    cycle_f = cycle_int.astype(jnp.float32)

    def cycle_row(block):
        return jnp.einsum("kac,kqc->aq", block.astype(jnp.float32), cycle_f, precision=lax.Precision.HIGHEST)

    cycle_term = lax.map(cycle_row, new_amps)
    return new_amps, cycle_term
```

```python
import jax
import jax.numpy as jnp
from jax import lax
from jax.experimental import pallas as pl
from jax.experimental.pallas import tpu as pltpu
from jax.sharding import PartitionSpec as P

MESH = pl.DeviceIdType.MESH
F32 = jnp.float32
BF16 = jnp.bfloat16
NX, NY, NZ = 4, 4, 12
NA, NB_, ND, NK, NQ = 10, 120, 120, 60, 64
CH = 5
KD = 2 * ND


def kernel(
    amp_ref, lad_ref, cyc_hbm, irr_s, ene_s, irr_ref, occ_ref, ene_ref,
    out_ref, z_ref,
    vec_f, vec_i, shard, sh_all, lt, a_f, a_b, nb, rb, of, cyc, crot, zp, zr,
    cyc_sem, own_sem, s1_send, s1_recv, s2_send, s2_recv, x_send, x_recv, e_send, e_recv, z_send, z_recv,
):
    row = lax.axis_index("row")
    col = lax.axis_index("col")
    x = lax.axis_index("dep")
    z = row // 4
    y = row % 4
    yh = col // 2
    core = col % 2

    def dev(zz, yy, cc, xx):
        return (zz * 4 + yy, cc, xx)

    r12 = 4 * (z % 3) + y
    xt = r12 // 3
    s_mine = r12 % 3
    ip_mine = z // 3
    s_here = (x + y) % 4
    z_off = (3 * x + s_here) // 4
    relay = s_here < 3

    left = (x + 3) % 4
    right = (x + 1) % 4
    diag = (x + 2) % 4

    barrier = pltpu.get_barrier_semaphore()

    def signal(d):
        pl.semaphore_signal(barrier, inc=1, device_id=d, device_id_type=MESH)

    @pl.when(relay)
    def _():
        def go(n, carry):
            i4 = n // 4
            xx = n % 4
            zz = 3 * i4 + z_off

            @pl.when(jnp.logical_or(zz != z, xx != x))
            def _():
                signal(dev(zz, y, col, xx))

            return carry

        lax.fori_loop(0, 16, go, 0)

    for t in range(1, 4):
        signal(dev(z, (y + t) % 4, col, x))
    signal(dev(z, y, col, left))
    signal(dev(z, y, col, right))
    for t in range(1, 4):
        signal(dev(z, y, (col + t) % 4, x))

    cyc_copy = pltpu.make_async_copy(cyc_hbm, cyc, cyc_sem)
    cyc_copy.start()

    raw = amp_ref[...]
    wide = jnp.concatenate(
        [raw[:, 0, :].astype(F32), raw[:, 1, :].astype(F32), jnp.zeros((20, 16), F32)], axis=1
    )
    gap = jnp.zeros((4, 128), F32)
    shard[...] = jnp.concatenate([wide[:, :128], gap, wide[:, 128:], gap], axis=0).astype(BF16)

    vec_f[...] = jnp.zeros_like(vec_f)
    vec_i[...] = jnp.zeros_like(vec_i)
    vec_f[0:1, 0:480] = ene_ref[...]
    vec_f[1:2, 0:60] = occ_ref[...]
    vec_i[0:1, 0:480] = irr_ref[...]
    lane = lax.broadcasted_iota(jnp.int32, (1, 128), 1)
    edge = 120 - 8 * col
    prev = jnp.maximum(col - 1, 0)
    at = pl.multiple_of(col * 128, 128)
    before = pl.multiple_of(prev * 128, 128)
    ene_b = jnp.where(lane < edge, vec_f[0:1, pl.ds(at, 128)], vec_f[0:1, pl.ds(before, 128)])
    irr_b = jnp.where(lane < edge, vec_i[0:1, pl.ds(at, 128)], vec_i[0:1, pl.ds(before, 128)])
    ii = lax.broadcasted_iota(jnp.int32, (ND, 512), 0)
    jj = lax.broadcasted_iota(jnp.int32, (ND, 512), 1)
    irr_d = jnp.sum(jnp.where(jj == ii + ND * x, vec_i[0:1, :].astype(F32), 0.0), axis=1, keepdims=True).astype(jnp.int32)
    pi = lax.broadcasted_iota(jnp.int32, (256, 128), 0)
    pj = lax.broadcasted_iota(jnp.int32, (256, 128), 1)
    occ_row = vec_f[1:2, 0:128]
    occ_i = jnp.sum(jnp.where(pj == (pi // 64) * 4 + x, occ_row, 0.0), axis=1, keepdims=True)
    occ_k = jnp.sum(jnp.where(pj == pi % 64, occ_row, 0.0), axis=1, keepdims=True)
    pair_occ = occ_i + occ_k

    sr = lax.broadcasted_iota(jnp.int32, (2 * NB_, 256), 0)
    sc = lax.broadcasted_iota(jnp.int32, (2 * NB_, 256), 1)
    want_b = (sc % 128 + 8 * col) % 128
    pick = jnp.where(sr == 2 * want_b + sc // 128, 1.0, 0.0).astype(BF16)

    def prep(a, carry):
        block = lad_ref[pl.ds(pl.multiple_of(a * 240, 240), 240), :]
        got = lax.dot_general(block, pick, (((0,), (0,)), ((), ())), preferred_element_type=F32)
        ab = jnp.bitwise_xor(irr_b, irr_s[row * NA + a])
        both = []
        for c in range(2):
            keep = jnp.bitwise_xor(ab, irr_s[c]) == irr_d
            both.append(jnp.where(keep, got[:, c * 128:(c + 1) * 128], 0.0))
        lt[x, a] = jnp.concatenate(both, axis=0).astype(BF16)
        return carry

    lax.fori_loop(0, NA, prep, 0)
    a_f[...] = jnp.zeros_like(a_f)

    pl.semaphore_wait(barrier, 8 + 12 - jnp.where(xt == x, 1, 0))

    def s1_copy(zz):
        return pltpu.make_async_remote_copy(
            src_ref=shard, dst_ref=sh_all.at[s_mine, ip_mine, x],
            send_sem=s1_send.at[zz], recv_sem=s1_recv.at[ip_mine, x],
            device_id=dev(zz, y, col, xt), device_id_type=MESH,
        )

    def s1_here(zz):
        return jnp.logical_and(zz == z, xt == x)

    def s1_go(n, carry):
        zz = (z + jnp.where(n % 2 == 0, 6 - n // 2, 12 - 5 + n // 2)) % 12

        @pl.when(jnp.logical_not(s1_here(zz)))
        def _():
            s1_copy(zz).start()

        return carry

    lax.fori_loop(0, 12, s1_go, 0)

    @pl.when(xt == x)
    def _():
        pltpu.make_async_copy(shard, sh_all.at[s_mine, ip_mine, x], own_sem).start()

    def x_own(j, side):
        return pltpu.make_async_remote_copy(
            src_ref=lt.at[x, pl.ds(2 * j, 2)], dst_ref=lt.at[x, pl.ds(2 * j, 2)],
            send_sem=x_send.at[side, j], recv_sem=x_recv.at[side, j],
            device_id=dev(z, y, col, left if side == 0 else right), device_id_type=MESH,
        )

    def x_fwd(j, side):
        owner = right if side == 0 else left
        a = 2 * j + (1 if side == 0 else 0)
        return pltpu.make_async_remote_copy(
            src_ref=lt.at[owner, a], dst_ref=lt.at[owner, a],
            send_sem=x_send.at[2 + side, j], recv_sem=x_recv.at[2 + side, j],
            device_id=dev(z, y, col, left if side == 0 else right), device_id_type=MESH,
        )

    for j in range(3):
        x_own(j, 0).start()
        x_own(j, 1).start()

    cyc_copy.wait()
    lane3 = lax.broadcasted_iota(jnp.int32, (1, 1, 128), 2)
    for t in range(4):
        @pl.when(col == t)
        def _():
            def rot(k, carry):
                lo = max(t - 1, 0) * 128
                if t < 3:
                    here = cyc[pl.ds(k, 1), :, t * 128:(t + 1) * 128]
                else:
                    here = jnp.concatenate(
                        [cyc[pl.ds(k, 1), :, 384:480], cyc[pl.ds(k, 1), :, 352:384]], axis=2
                    )
                there = cyc[pl.ds(k, 1), :, lo:lo + 128]
                crot[pl.ds(k, 1)] = jnp.where(lane3 < 120 - 8 * t, here, there)
                return carry

            lax.fori_loop(0, NK, rot, 0)

    def s2_copy(t, h):
        half = (1 - yh) if h == 0 else yh
        return pltpu.make_async_remote_copy(
            src_ref=sh_all.at[s_here, pl.ds(2 * half, 2)], dst_ref=sh_all.at[s_here, pl.ds(2 * half, 2)],
            send_sem=s2_send.at[t - 1, h], recv_sem=s2_recv.at[s_here, h],
            device_id=dev(z, (y + t) % 4, col, x), device_id_type=MESH,
        )

    @pl.when(relay)
    def _():
        def got(n, carry):
            i4 = n // 4
            xx = n % 4
            zz = 3 * i4 + z_off

            @pl.when(jnp.logical_or(zz != z, xx != x))
            def _():
                pltpu.make_async_remote_copy(
                    src_ref=shard, dst_ref=sh_all.at[s_here, i4, xx],
                    send_sem=s1_send.at[0], recv_sem=s1_recv.at[i4, xx],
                    device_id=dev(z, y, col, x), device_id_type=MESH,
                ).wait_recv()

            return carry

        lax.fori_loop(0, 16, got, 0)

    @pl.when(xt == x)
    def _():
        pltpu.make_async_copy(shard, sh_all.at[s_mine, ip_mine, x], own_sem).wait()

    @pl.when(relay)
    def _():
        for h in range(2):
            for t in (2, 1, 3):
                s2_copy(t, h).start()

    def forward(j):
        x_own(j, 0).wait_recv()
        x_own(j, 1).wait_recv()
        x_fwd(j, 0).start()
        x_fwd(j, 1).start()
        if j + 3 < CH:
            x_own(j + 3, 0).start()
            x_own(j + 3, 1).start()

    forward(0)
    forward(1)

    def s2_wait(s, h):
        half = (1 - yh) if h == 0 else yh
        pltpu.make_async_remote_copy(
            src_ref=sh_all.at[s, pl.ds(2 * half, 2)], dst_ref=sh_all.at[s, pl.ds(2 * half, 2)],
            send_sem=s2_send.at[0, h], recv_sem=s2_recv.at[s, h],
            device_id=dev(z, y, col, x), device_id_type=MESH,
        ).wait_recv()

    for h in range(2):
        for s in range(3):
            @pl.when(s_here != s)
            def _():
                s2_wait(s, h)

    for xx in range(4):
        for i4 in range(4):
            for s in range(3):
                got = sh_all[s, i4, xx].astype(F32)
                top = i4 * 64 + s * 20
                a_f[top:top + 20, 0:128] = got[0:20]
                a_f[top:top + 20, 128:256] = got[24:44]
        a_b[xx] = a_f[...].astype(BF16)

    partners = [(2, 0), (2, 1), (0, 1)]

    def e_copy(p, j):
        dh, dc = partners[p]
        to = ((yh * 2 + dh) % 4) + (core + dc) % 2
        return pltpu.make_async_remote_copy(
            src_ref=nb.at[to, pl.ds(2 * j, 2)], dst_ref=rb.at[col, pl.ds(2 * j, 2)],
            send_sem=e_send.at[p, j], recv_sem=e_recv.at[p, j],
            device_id=dev(z, y, to, x), device_id_type=MESH,
        )

    def e_wait(p, j):
        dh, dc = partners[p]
        frm = ((yh * 2 + dh) % 4) + (core + dc) % 2
        pltpu.make_async_remote_copy(
            src_ref=nb.at[frm, pl.ds(2 * j, 2)], dst_ref=rb.at[frm, pl.ds(2 * j, 2)],
            send_sem=e_send.at[p, j], recv_sem=e_recv.at[p, j],
            device_id=dev(z, y, frm, x), device_id_type=MESH,
        ).wait_recv()

    for j in range(CH):
        if j + 2 < CH:
            forward(j + 2)
        x_fwd(j, 0).wait_recv()
        x_fwd(j, 1).wait_recv()
        total = None
        for xx in range(4):
            w = jnp.concatenate([lt[xx, 2 * j], lt[xx, 2 * j + 1]], axis=1)
            term = jnp.dot(a_b[xx, :, 0:KD], w, preferred_element_type=F32)
            total = term if total is None else total + term
        for h in range(2):
            a = 2 * j + h
            denom = (ene_s[row * NA + a] + ene_b) - pair_occ
            new = (total[:, h * 128:(h + 1) * 128] / denom).astype(BF16)
            for i4 in range(4):
                nb[i4, a] = new[i4 * 64:(i4 + 1) * 64]
            of[a * 256:(a + 1) * 256, :] = new.astype(F32)
        for p in range(3):
            e_copy(p, j).start()

    rb[pl.ds(col, 1)] = nb[pl.ds(col, 1)]

    def cycle(k, acc):
        rows = []
        for i4 in range(4):
            rows.append(of[pl.ds(i4 * 64 + k, 10, stride=256), :])
            rows.append(jnp.zeros((6, 128), F32))
        left_op = jnp.concatenate(rows, axis=0).astype(BF16)
        return acc + lax.dot_general(left_op, crot[k], (((1,), (1,)), ((), ())), preferred_element_type=F32)

    zsum = lax.fori_loop(0, NK, cycle, jnp.zeros((64, NQ), F32))
    zw = jnp.concatenate([zsum, jnp.zeros((64, 64), F32)], axis=1)
    for i4 in range(4):
        zp[i4] = zw[i4 * 16:(i4 + 1) * 16]
    zr[pl.ds(col, 1)] = zp[pl.ds(col, 1)]

    def z_copy(p):
        dh, dc = partners[p]
        to = ((yh * 2 + dh) % 4) + (core + dc) % 2
        return pltpu.make_async_remote_copy(
            src_ref=zp.at[to], dst_ref=zr.at[col],
            send_sem=z_send.at[p], recv_sem=z_recv.at[p],
            device_id=dev(z, y, to, x), device_id_type=MESH,
        )

    def z_wait(p):
        dh, dc = partners[p]
        frm = ((yh * 2 + dh) % 4) + (core + dc) % 2
        pltpu.make_async_remote_copy(
            src_ref=zp.at[frm], dst_ref=zr.at[frm],
            send_sem=z_send.at[p], recv_sem=z_recv.at[p],
            device_id=dev(z, y, frm, x), device_id_type=MESH,
        ).wait_recv()

    for p in range(3):
        z_copy(p).start()

    lane_o = lax.broadcasted_iota(jnp.int32, (1, 128), 1)
    for j in range(CH):
        for p in range(3):
            e_wait(p, j)
        for h in range(2):
            a = 2 * j + h
            for t in range(3):
                tile = jnp.where(lane_o < 120 - 8 * t, rb[t, a], rb[t + 1, a])
                out_ref[a, :, t * 128:(t + 1) * 128] = tile[:NK]
            out_ref[a, :, 384:480] = rb[3, a][:NK, :96]

    for p in range(3):
        z_wait(p)
    zt = (zr[0] + zr[1]) + (zr[2] + zr[3])
    z_ref[...] = zt[:NA, :NQ]

    def s1_done(zz, carry):
        @pl.when(jnp.logical_not(s1_here(zz)))
        def _():
            s1_copy(zz).wait_send()

        return carry

    lax.fori_loop(0, 12, s1_done, 0)

    @pl.when(relay)
    def _():
        for h in range(2):
            for t in range(1, 4):
                s2_copy(t, h).wait_send()

    for j in range(CH):
        for side in range(2):
            x_own(j, side).wait_send()
            x_fwd(j, side).wait_send()
        for p in range(3):
            e_copy(p, j).wait_send()
    for p in range(3):
        z_copy(p).wait_send()


def on_device(amp_old, ladder_int, cycle_int, virt_irrep, occ_energy, virt_energy):
    vmem = pl.BlockSpec(memory_space=pltpu.VMEM)
    smem = pl.BlockSpec(memory_space=pltpu.SMEM)
    dma = pltpu.SemaphoreType.DMA
    lad = ladder_int.reshape(2 * NA * NB_, ND)
    amps, cyc = pl.pallas_call(
        kernel,
        name="ladder",
        out_shape=(
            jax.ShapeDtypeStruct((NA, NK, 480), BF16),
            jax.ShapeDtypeStruct((NA, NQ), F32),
        ),
        in_specs=[vmem, vmem, pl.BlockSpec(memory_space=pl.ANY), smem, smem, vmem, vmem, vmem],
        out_specs=(vmem, vmem),
        scratch_shapes=[
            pltpu.VMEM((8, 512), F32),
            pltpu.VMEM((8, 512), jnp.int32),
            pltpu.VMEM((48, 128), BF16),
            pltpu.VMEM((3, 4, 4, 48, 128), BF16),
            pltpu.VMEM((4, NA, KD, 128), BF16),
            pltpu.VMEM((256, 256), F32),
            pltpu.VMEM((4, 256, 256), BF16),
            pltpu.VMEM((4, NA, 64, 128), BF16),
            pltpu.VMEM((4, NA, 64, 128), BF16),
            pltpu.VMEM((NA * 256, 128), F32),
            pltpu.VMEM((NK, NQ, 480), BF16),
            pltpu.VMEM((NK, NQ, 128), BF16),
            pltpu.VMEM((4, 16, 128), F32),
            pltpu.VMEM((4, 16, 128), F32),
            dma, dma, dma((12,)), dma((4, 4)), dma((3, 2)), dma((3, 2)),
            dma((4, CH)), dma((4, CH)), dma((3, CH)), dma((3, CH)), dma((3,)), dma((3,)),
        ],
        compiler_params=pltpu.CompilerParams(
            collective_id=0, has_side_effects=True, vmem_limit_bytes=48 << 20
        ),
    )(
        amp_old, lad, cycle_int, virt_irrep, virt_energy,
        virt_irrep.reshape(1, 480), occ_energy.reshape(1, 60), virt_energy.reshape(1, 480),
    )
    return amps.transpose(1, 0, 2)[None], cyc[None]


def solution(mesh):
    placed = (P("row", None, "dep"), P("row", "col", None, "dep"), P(), P(), P(), P())
    return jax.shard_map(
        on_device,
        mesh=mesh,
        in_specs=placed,
        out_specs=(P(("col", "dep"), None, "row", None), P(("col", "dep"), "row", None)),
        check_vma=False,
    )
```

```python
import jax
import jax.numpy as jnp
from jax import lax
from jax.experimental import pallas as pl
from jax.experimental.pallas import tpu as pltpu
from jax.sharding import PartitionSpec as P

MESH = pl.DeviceIdType.MESH
F32 = jnp.float32
BF16 = jnp.bfloat16
NX, NY, NZ = 4, 4, 12
NA, NB_, ND, NK, NQ = 10, 120, 120, 60, 64
CH = 5
KD = 2 * ND


def kernel(
    amp_hbm, lad_hbm, cyc_hbm, irr_hbm, occ_hbm, ene_hbm,
    out_ref, z_ref,
    amp_ref, lad_ref, irr_ref, occ_ref, ene_ref, vec_f, vec_i, shard, sh_all, lt, a_f, a_b, nb, rb, of, cyc, crot, zp, zr,
    in_sem, own_sem, s1_send, s1_recv, s2_send, s2_recv, b_send, b_recv, x_send, x_recv, e_send, e_recv, z_send, z_recv,
):
    row = lax.axis_index("row")
    col = lax.axis_index("col")
    x = lax.axis_index("dep")
    z = row // 4
    y = row % 4
    yh = col // 2
    core = col % 2

    def dev(zz, yy, cc, xx):
        return (zz * 4 + yy, cc, xx)

    r12 = 4 * (z % 3) + y
    xt = r12 // 3
    s_mine = r12 % 3
    ip_mine = z // 3
    s_here = (x + y) % 4
    z_off = (3 * x + s_here) // 4
    relay = s_here < 3

    left = (x + 3) % 4
    right = (x + 1) % 4
    diag = (x + 2) % 4

    barrier = pltpu.get_barrier_semaphore()

    def parity(s):
        return (core + (3 * x + s) // 4 + z) % 2

    def signal(d):
        pl.semaphore_signal(barrier, inc=1, device_id=d, device_id_type=MESH)

    @pl.when(relay)
    def _():
        def go(n, carry):
            zz = 3 * (2 * (n // 4) + parity(s_here)) + z_off
            xx = n % 4

            @pl.when(jnp.logical_or(zz != z, xx != x))
            def _():
                signal(dev(zz, y, col, xx))

            return carry

        lax.fori_loop(0, 8, go, 0)

    for t in range(1, 4):
        signal(dev(z, (y + t) % 4, col, x))
    signal(dev(z, y, col, left))
    signal(dev(z, y, col, right))
    for t in range(1, 4):
        signal(dev(z, y, (col + t) % 4, x))

    loads = [
        pltpu.make_async_copy(src, dst, in_sem.at[n])
        for n, (src, dst) in enumerate(
            [(amp_hbm, amp_ref), (irr_hbm, irr_ref), (occ_hbm, occ_ref), (ene_hbm, ene_ref), (lad_hbm, lad_ref), (cyc_hbm, cyc)]
        )
    ]
    for copy in loads:
        copy.start()
    cyc_copy = loads[5]
    a_f[...] = jnp.zeros_like(a_f)
    of[NA * 256:, :] = jnp.zeros((6 * 256, 128), F32)
    for copy in loads[:4]:
        copy.wait()

    raw = amp_ref[...]
    wide = jnp.concatenate(
        [raw[:, 0, :].astype(F32), raw[:, 1, :].astype(F32), jnp.zeros((20, 16), F32)], axis=1
    )
    gap = jnp.zeros((4, 128), F32)
    shard[...] = jnp.concatenate([wide[:, :128], gap, wide[:, 128:], gap], axis=0).astype(BF16)

    vec_f[...] = jnp.zeros_like(vec_f)
    vec_i[...] = jnp.zeros_like(vec_i)
    vec_f[0:1, 0:480] = ene_ref[...]
    vec_f[1:2, 0:60] = occ_ref[...]
    vec_i[0:1, 0:480] = irr_ref[...]
    lane = lax.broadcasted_iota(jnp.int32, (1, 128), 1)
    edge = 120 - 8 * col
    prev = jnp.maximum(col - 1, 0)
    at = pl.multiple_of(col * 128, 128)
    before = pl.multiple_of(prev * 128, 128)
    ene_b = jnp.where(lane < edge, vec_f[0:1, pl.ds(at, 128)], vec_f[0:1, pl.ds(before, 128)])
    irr_b = jnp.where(lane < edge, vec_i[0:1, pl.ds(at, 128)], vec_i[0:1, pl.ds(before, 128)])
    ii = lax.broadcasted_iota(jnp.int32, (ND, 512), 0)
    jj = lax.broadcasted_iota(jnp.int32, (ND, 512), 1)
    irr_d = jnp.sum(jnp.where(jj == ii + ND * x, vec_i[0:1, :].astype(F32), 0.0), axis=1, keepdims=True).astype(jnp.int32)
    pi = lax.broadcasted_iota(jnp.int32, (128, 128), 0)
    pj = lax.broadcasted_iota(jnp.int32, (128, 128), 1)
    occ_row = vec_f[1:2, 0:128]
    wide_lane = lax.broadcasted_iota(jnp.int32, (1, 512), 1)

    def ene_of(a):
        return jnp.sum(jnp.where(wide_lane == row * NA + a, vec_f[0:1, :], 0.0), axis=1, keepdims=True)

    def irr_of(n):
        picked = jnp.sum(jnp.where(wide_lane == n, vec_i[0:1, :].astype(F32), 0.0), axis=1, keepdims=True)
        return picked.astype(jnp.int32)

    irr_c = [irr_of(c) for c in range(2)]

    def occ_i_of(half):
        return jnp.sum(jnp.where(pj == (2 * half + pi // 64) * 4 + x, occ_row, 0.0), axis=1, keepdims=True)

    occ_k = jnp.sum(jnp.where(pj == pi % 64, occ_row, 0.0), axis=1, keepdims=True)
    occ_half = [occ_i_of(1 - yh) + occ_k, occ_i_of(yh) + occ_k]

    sr = lax.broadcasted_iota(jnp.int32, (2 * NB_, 256), 0)
    sc = lax.broadcasted_iota(jnp.int32, (2 * NB_, 256), 1)
    want_b = (sc % 128 + 8 * col) % 128
    pick = jnp.where(sr == 2 * want_b + sc // 128, 1.0, 0.0).astype(BF16)

    def prep(a, carry):
        block = lad_ref[pl.ds(pl.multiple_of(a * 240, 240), 240), :]
        got = lax.dot_general(block, pick, (((0,), (0,)), ((), ())), preferred_element_type=F32)
        ab = jnp.bitwise_xor(irr_b, irr_of(row * NA + a))
        both = []
        for c in range(2):
            keep = jnp.bitwise_xor(ab, irr_c[c]) == irr_d
            both.append(jnp.where(keep, got[:, c * 128:(c + 1) * 128], 0.0))
        lt[x, a] = jnp.concatenate(both, axis=0).astype(BF16)
        return carry

    loads[4].wait()
    lax.fori_loop(0, NA, prep, 0)

    pl.semaphore_wait(barrier, 8 + 6 - jnp.where(jnp.logical_and(xt == x, core == 0), 1, 0))

    def s1_plane(n):
        even = jnp.where(n == 0, 6, jnp.where(n == 1, 8, jnp.where(n == 2, 4, jnp.where(n == 3, 10, jnp.where(n == 4, 2, 0)))))
        odd = jnp.where(n == 0, 5, jnp.where(n == 1, 7, jnp.where(n == 2, 3, jnp.where(n == 3, 9, jnp.where(n == 4, 1, 11)))))
        return (z + jnp.where(core == 0, even, odd)) % 12

    def s1_copy(n):
        zz = s1_plane(n)
        return pltpu.make_async_remote_copy(
            src_ref=shard, dst_ref=sh_all.at[s_mine, ip_mine, x],
            send_sem=s1_send.at[n], recv_sem=s1_recv.at[ip_mine, x],
            device_id=dev(zz, y, col, xt), device_id_type=MESH,
        )

    def s1_here(n):
        return jnp.logical_and(s1_plane(n) == z, xt == x)

    stays = jnp.logical_and(xt == x, core == 0)

    def s1_go(n, carry):
        @pl.when(jnp.logical_not(s1_here(n)))
        def _():
            s1_copy(n).start()

        return carry

    lax.fori_loop(0, 6, s1_go, 0)

    @pl.when(stays)
    def _():
        pltpu.make_async_copy(shard, sh_all.at[s_mine, ip_mine, x], own_sem).start()

    def x_own(j, side):
        return pltpu.make_async_remote_copy(
            src_ref=lt.at[x, pl.ds(2 * j, 2)], dst_ref=lt.at[x, pl.ds(2 * j, 2)],
            send_sem=x_send.at[side, j], recv_sem=x_recv.at[side, j],
            device_id=dev(z, y, col, left if side == 0 else right), device_id_type=MESH,
        )

    def x_fwd(j, side):
        owner = right if side == 0 else left
        a = 2 * j + (1 if side == 0 else 0)
        return pltpu.make_async_remote_copy(
            src_ref=lt.at[owner, a], dst_ref=lt.at[owner, a],
            send_sem=x_send.at[2 + side, j], recv_sem=x_recv.at[2 + side, j],
            device_id=dev(z, y, col, left if side == 0 else right), device_id_type=MESH,
        )

    for j in range(3):
        x_own(j, 0).start()
        x_own(j, 1).start()

    cyc_copy.wait()
    lane3 = lax.broadcasted_iota(jnp.int32, (1, 1, 128), 2)
    for t in range(4):
        @pl.when(col == t)
        def _():
            def rot(m, carry):
                lo = max(t - 1, 0) * 128
                for u in range(2):
                    k = 2 * m + u
                    if t < 3:
                        here = cyc[pl.ds(k, 1), :, t * 128:(t + 1) * 128]
                    else:
                        here = jnp.concatenate(
                            [cyc[pl.ds(k, 1), :, 384:480], cyc[pl.ds(k, 1), :, 352:384]], axis=2
                        )
                    there = cyc[pl.ds(k, 1), :, lo:lo + 128]
                    crot[pl.ds(m, 1), :, u * 128:(u + 1) * 128] = jnp.where(lane3 < 120 - 8 * t, here, there)
                return carry

            lax.fori_loop(0, NK // 2, rot, 0)

    def unit(s, h, mine):
        half = (1 - yh) if h == 0 else yh
        share = parity(s) if mine else 1 - parity(s)
        return sh_all.at[s, 2 * half + share]

    def s2_copy(t, h):
        return pltpu.make_async_remote_copy(
            src_ref=unit(s_here, h, True), dst_ref=unit(s_here, h, True),
            send_sem=s2_send.at[t - 1, h], recv_sem=s2_recv.at[s_here, h],
            device_id=dev(z, (y + t) % 4, col, x), device_id_type=MESH,
        )

    def s2_wait(s, h):
        return pltpu.make_async_remote_copy(
            src_ref=unit(s, h, True), dst_ref=unit(s, h, True),
            send_sem=s2_send.at[0, h], recv_sem=s2_recv.at[s, h],
            device_id=dev(z, (y + 1) % 4, col, x), device_id_type=MESH,
        )

    other = 2 * yh + 1 - core

    def sib_copy(s, h):
        return pltpu.make_async_remote_copy(
            src_ref=unit(s, h, True), dst_ref=unit(s, h, True),
            send_sem=b_send.at[s, h], recv_sem=b_recv.at[s, h],
            device_id=dev(z, y, other, x), device_id_type=MESH,
        )

    def sib_wait(s, h):
        return pltpu.make_async_remote_copy(
            src_ref=unit(s, h, False), dst_ref=unit(s, h, False),
            send_sem=b_send.at[s, h], recv_sem=b_recv.at[s, h],
            device_id=dev(z, y, other, x), device_id_type=MESH,
        )

    def forward(j):
        x_own(j, 0).wait_recv()
        x_own(j, 1).wait_recv()
        x_fwd(j, 0).start()
        x_fwd(j, 1).start()
        if j + 3 < CH:
            x_own(j + 3, 0).start()
            x_own(j + 3, 1).start()

    forward(0)

    @pl.when(stays)
    def _():
        pltpu.make_async_copy(shard, sh_all.at[s_mine, ip_mine, x], own_sem).wait()

    @pl.when(relay)
    def _():
        for h in range(2):
            half = (1 - yh) if h == 0 else yh
            i4 = 2 * half + parity(s_here)
            zz = 3 * i4 + z_off

            def got(xx, carry):
                @pl.when(jnp.logical_or(zz != z, xx != x))
                def _():
                    pltpu.make_async_remote_copy(
                        src_ref=shard, dst_ref=sh_all.at[s_here, i4, xx],
                        send_sem=s1_send.at[0], recv_sem=s1_recv.at[i4, xx],
                        device_id=dev(z, y, other, x), device_id_type=MESH,
                    ).wait_recv()

                return carry

            lax.fori_loop(0, 4, got, 0)
            for t in (2, 1, 3):
                s2_copy(t, h).start()
            sib_copy(s_here, h).start()

    def pass_on(h):
        for s in range(3):
            @pl.when(s_here != s)
            def _():
                s2_wait(s, h).wait_recv()
                sib_copy(s, h).start()

    def operand(h):
        half = (1 - yh) if h == 0 else yh
        for s in range(3):
            sib_wait(s, h).wait_recv()
        base = pl.multiple_of(half * 128, 128)
        for xx in range(4):
            for n in range(2):
                for s in range(3):
                    got = sh_all[s, 2 * half + n, xx].astype(F32)
                    top = n * 64 + s * 20
                    a_f[top:top + 20, 0:128] = got[0:20]
                    a_f[top:top + 20, 128:256] = got[24:44]
            a_b[xx, pl.ds(base, 128), :] = a_f[...].astype(BF16)

    forward(1)
    pass_on(0)
    pass_on(1)
    forward(2)
    operand(0)

    partners = [(2, 0), (2, 1), (0, 1)]

    def e_copy(p, j):
        dh, dc = partners[p]
        to = ((yh * 2 + dh) % 4) + (core + dc) % 2
        return pltpu.make_async_remote_copy(
            src_ref=nb.at[to, pl.ds(2 * j, 2)], dst_ref=rb.at[col, pl.ds(2 * j, 2)],
            send_sem=e_send.at[p, j], recv_sem=e_recv.at[p, j],
            device_id=dev(z, y, to, x), device_id_type=MESH,
        )

    def e_wait(p, j):
        dh, dc = partners[p]
        frm = ((yh * 2 + dh) % 4) + (core + dc) % 2
        pltpu.make_async_remote_copy(
            src_ref=nb.at[frm, pl.ds(2 * j, 2)], dst_ref=rb.at[frm, pl.ds(2 * j, 2)],
            send_sem=e_send.at[p, j], recv_sem=e_recv.at[p, j],
            device_id=dev(z, y, frm, x), device_id_type=MESH,
        ).wait_recv()

    def block(j, h):
        half = (1 - yh) if h == 0 else yh
        base = pl.multiple_of(half * 128, 128)
        total = None
        for xx in range(4):
            w = jnp.concatenate([lt[xx, 2 * j], lt[xx, 2 * j + 1]], axis=1)
            term = jnp.dot(a_b[xx, pl.ds(base, 128), 0:KD], w, preferred_element_type=F32)
            total = term if total is None else total + term
        occ = occ_half[h]
        for g in range(2):
            a = 2 * j + g
            denom = (ene_of(a) + ene_b) - occ
            new = (total[:, g * 128:(g + 1) * 128] / denom).astype(BF16)
            nb[2 * half, a] = new[0:64]
            nb[2 * half + 1, a] = new[64:128]
            of[pl.ds(pl.multiple_of(a * 256 + half * 128, 128), 128), :] = new.astype(F32)
        for p in ((0, 1) if h == 0 else (2,)):
            e_copy(p, j).start()

    def diag_in(j):
        x_fwd(j, 0).wait_recv()
        x_fwd(j, 1).wait_recv()

    diag_in(0)
    block(0, 0)
    diag_in(1)
    block(1, 0)
    forward(3)
    operand(1)
    block(0, 1)
    block(1, 1)
    diag_in(2)
    block(2, 0)
    block(2, 1)
    forward(4)
    for j in range(3, CH):
        diag_in(j)
        block(j, 0)
        block(j, 1)

    rb[pl.ds(col, 1)] = nb[pl.ds(col, 1)]

    def cycle(m, acc):
        parts = []
        for u in range(2):
            rows = [of[pl.ds(i4 * 64 + 2 * m + u, 16, stride=256), :] for i4 in range(4)]
            parts.append(jnp.concatenate(rows, axis=0).astype(BF16))
        left_op = jnp.concatenate(parts, axis=1)
        return acc + lax.dot_general(left_op, crot[m], (((1,), (1,)), ((), ())), preferred_element_type=F32)

    zsum = lax.fori_loop(0, NK // 2, cycle, jnp.zeros((64, NQ), F32), unroll=5)
    zw = jnp.concatenate([zsum, jnp.zeros((64, 64), F32)], axis=1)
    for i4 in range(4):
        zp[i4] = zw[i4 * 16:(i4 + 1) * 16]
    zr[pl.ds(col, 1)] = zp[pl.ds(col, 1)]

    def z_copy(p):
        dh, dc = partners[p]
        to = ((yh * 2 + dh) % 4) + (core + dc) % 2
        return pltpu.make_async_remote_copy(
            src_ref=zp.at[to], dst_ref=zr.at[col],
            send_sem=z_send.at[p], recv_sem=z_recv.at[p],
            device_id=dev(z, y, to, x), device_id_type=MESH,
        )

    def z_wait(p):
        dh, dc = partners[p]
        frm = ((yh * 2 + dh) % 4) + (core + dc) % 2
        pltpu.make_async_remote_copy(
            src_ref=zp.at[frm], dst_ref=zr.at[frm],
            send_sem=z_send.at[p], recv_sem=z_recv.at[p],
            device_id=dev(z, y, frm, x), device_id_type=MESH,
        ).wait_recv()

    for p in range(3):
        z_copy(p).start()

    lane_o = lax.broadcasted_iota(jnp.int32, (1, 128), 1)
    for j in range(CH):
        for p in range(3):
            e_wait(p, j)
        for h in range(2):
            a = 2 * j + h
            for t in range(3):
                tile = jnp.where(lane_o < 120 - 8 * t, rb[t, a], rb[t + 1, a])
                out_ref[a, :, t * 128:(t + 1) * 128] = tile[:NK]
            out_ref[a, :, 384:480] = rb[3, a][:NK, :96]

    for p in range(3):
        z_wait(p)
    zt = (zr[0] + zr[1]) + (zr[2] + zr[3])
    z_ref[...] = zt[:NA, :NQ]

    def s1_done(n, carry):
        @pl.when(jnp.logical_not(s1_here(n)))
        def _():
            s1_copy(n).wait_send()

        return carry

    lax.fori_loop(0, 6, s1_done, 0)

    @pl.when(relay)
    def _():
        for h in range(2):
            for t in range(1, 4):
                s2_copy(t, h).wait_send()

    for h in range(2):
        for s in range(3):
            sib_copy(s, h).wait_send()

    for j in range(CH):
        for side in range(2):
            x_own(j, side).wait_send()
            x_fwd(j, side).wait_send()
        for p in range(3):
            e_copy(p, j).wait_send()
    for p in range(3):
        z_copy(p).wait_send()


def on_device(amp_old, ladder_int, cycle_int, virt_irrep, occ_energy, virt_energy):
    vmem = pl.BlockSpec(memory_space=pltpu.VMEM)
    hbm = pl.BlockSpec(memory_space=pltpu.HBM)
    dma = pltpu.SemaphoreType.DMA
    lad = ladder_int.reshape(2 * NA * NB_, ND)
    amps, cyc = pl.pallas_call(
        kernel,
        name="ladder",
        out_shape=(
            jax.ShapeDtypeStruct((NA, NK, 480), BF16),
            jax.ShapeDtypeStruct((NA, NQ), F32),
        ),
        in_specs=[hbm] * 6,
        out_specs=(vmem, vmem),
        scratch_shapes=[
            pltpu.VMEM((20, 2, ND), BF16),
            pltpu.VMEM((2 * NA * NB_, ND), BF16),
            pltpu.VMEM((1, 480), jnp.int32),
            pltpu.VMEM((1, NK), F32),
            pltpu.VMEM((1, 480), F32),
            pltpu.VMEM((8, 512), F32),
            pltpu.VMEM((8, 512), jnp.int32),
            pltpu.VMEM((48, 128), BF16),
            pltpu.VMEM((3, 4, 4, 48, 128), BF16),
            pltpu.VMEM((4, NA, KD, 128), BF16),
            pltpu.VMEM((128, 256), F32),
            pltpu.VMEM((4, 256, 256), BF16),
            pltpu.VMEM((4, NA, 64, 128), BF16),
            pltpu.VMEM((4, NA, 64, 128), BF16),
            pltpu.VMEM((16 * 256, 128), F32),
            pltpu.VMEM((NK, NQ, 480), BF16),
            pltpu.VMEM((NK // 2, NQ, 256), BF16),
            pltpu.VMEM((4, 16, 128), F32),
            pltpu.VMEM((4, 16, 128), F32),
            dma((6,)), dma, dma((6,)), dma((4, 4)), dma((3, 2)), dma((3, 2)), dma((3, 2)), dma((3, 2)),
            dma((4, CH)), dma((4, CH)), dma((3, CH)), dma((3, CH)), dma((3,)), dma((3,)),
        ],
        compiler_params=pltpu.CompilerParams(
            collective_id=0, has_side_effects=True, vmem_limit_bytes=60 << 20
        ),
    )(
        amp_old, lad, cycle_int,
        virt_irrep.reshape(1, 480), occ_energy.reshape(1, 60), virt_energy.reshape(1, 480),
    )
    return amps.transpose(1, 0, 2)[None], cyc[None]


def solution(mesh):
    placed = (P("row", None, "dep"), P("row", "col", None, "dep"), P(), P(), P(), P())
    return jax.shard_map(
        on_device,
        mesh=mesh,
        in_specs=placed,
        out_specs=(P(("col", "dep"), None, "row", None), P(("col", "dep"), "row", None)),
        check_vma=False,
    )
```

```python
import jax
import jax.numpy as jnp
from jax import lax
from jax.experimental import pallas as pl
from jax.experimental.pallas import tpu as pltpu
from jax.sharding import PartitionSpec as P

MESH = pl.DeviceIdType.MESH
F32 = jnp.float32
BF16 = jnp.bfloat16
NX, NY, NZ = 4, 4, 12
NA, NB_, ND, NK, NQ = 10, 120, 120, 60, 64
CH = 5
KD = 2 * ND


def kernel(
    amp_hbm, lad_hbm, cyc_hbm, irr_hbm, occ_hbm, ene_hbm,
    out_hbm, z_hbm,
    out_ref, z_ref, amp_ref, lad_ref, irr_ref, occ_ref, ene_ref, vec_f, vec_i, shard, sh_all, lt, a_f, a_b, nb, rb, of, cyc, crot, zp, zr,
    in_sem, out_sem, own_sem, s1_send, s1_recv, s2_send, s2_recv, b_send, b_recv, x_send, x_recv, e_send, e_recv, z_send, z_recv,
):
    row = lax.axis_index("row")
    col = lax.axis_index("col")
    x = lax.axis_index("dep")
    z = row // 4
    y = row % 4
    yh = col // 2
    core = col % 2

    def dev(zz, yy, cc, xx):
        return (zz * 4 + yy, cc, xx)

    r12 = 4 * (z % 3) + y
    xt = r12 // 3
    s_mine = r12 % 3
    ip_mine = z // 3
    s_here = (x + y) % 4
    z_off = (3 * x + s_here) // 4
    relay = s_here < 3

    left = (x + 3) % 4
    right = (x + 1) % 4
    diag = (x + 2) % 4

    barrier = pltpu.get_barrier_semaphore()

    def parity(s):
        return (core + (3 * x + s) // 4 + z) % 2

    def signal(d):
        pl.semaphore_signal(barrier, inc=1, device_id=d, device_id_type=MESH)

    @pl.when(relay)
    def _():
        def go(n, carry):
            zz = 3 * (2 * (n // 4) + parity(s_here)) + z_off
            xx = n % 4

            @pl.when(jnp.logical_or(zz != z, xx != x))
            def _():
                signal(dev(zz, y, col, xx))

            return carry

        lax.fori_loop(0, 8, go, 0)

    for t in range(1, 4):
        signal(dev(z, (y + t) % 4, col, x))
    signal(dev(z, y, col, left))
    signal(dev(z, y, col, right))
    for t in range(1, 4):
        signal(dev(z, y, (col + t) % 4, x))

    loads = [
        pltpu.make_async_copy(src, dst, in_sem.at[n])
        for n, (src, dst) in enumerate(
            [(amp_hbm, amp_ref), (irr_hbm, irr_ref), (occ_hbm, occ_ref), (ene_hbm, ene_ref), (lad_hbm, lad_ref), (cyc_hbm, cyc)]
        )
    ]
    for copy in loads:
        copy.start()
    cyc_copy = loads[5]
    loads[0].wait()

    raw = amp_ref[...]
    wide = jnp.concatenate(
        [raw[:, 0, :].astype(F32), raw[:, 1, :].astype(F32), jnp.zeros((20, 16), F32)], axis=1
    )
    gap = jnp.zeros((4, 128), F32)
    shard[...] = jnp.concatenate([wide[:, :128], gap, wide[:, 128:], gap], axis=0).astype(BF16)

    for copy in loads[1:4]:
        copy.wait()

    vec_f[...] = jnp.zeros_like(vec_f)
    vec_i[...] = jnp.zeros_like(vec_i)
    vec_f[0:1, 0:480] = ene_ref[...]
    vec_f[1:2, 0:60] = occ_ref[...]
    vec_i[0:1, 0:480] = irr_ref[...]
    lane = lax.broadcasted_iota(jnp.int32, (1, 128), 1)
    edge = 120 - 8 * col
    prev = jnp.maximum(col - 1, 0)
    at = pl.multiple_of(col * 128, 128)
    before = pl.multiple_of(prev * 128, 128)
    ene_b = jnp.where(lane < edge, vec_f[0:1, pl.ds(at, 128)], vec_f[0:1, pl.ds(before, 128)])
    irr_b = jnp.where(lane < edge, vec_i[0:1, pl.ds(at, 128)], vec_i[0:1, pl.ds(before, 128)])
    ii = lax.broadcasted_iota(jnp.int32, (ND, 512), 0)
    jj = lax.broadcasted_iota(jnp.int32, (ND, 512), 1)
    irr_d = jnp.sum(jnp.where(jj == ii + ND * x, vec_i[0:1, :].astype(F32), 0.0), axis=1, keepdims=True).astype(jnp.int32)
    wide_lane = lax.broadcasted_iota(jnp.int32, (1, 512), 1)

    def ene_of(a):
        return jnp.sum(jnp.where(wide_lane == row * NA + a, vec_f[0:1, :], 0.0), axis=1, keepdims=True)

    def irr_of(n):
        picked = jnp.sum(jnp.where(wide_lane == n, vec_i[0:1, :].astype(F32), 0.0), axis=1, keepdims=True)
        return picked.astype(jnp.int32)

    irr_c = [irr_of(c) for c in range(2)]

    sr = lax.broadcasted_iota(jnp.int32, (2 * NB_, 256), 0)
    sc = lax.broadcasted_iota(jnp.int32, (2 * NB_, 256), 1)
    want_b = (sc % 128 + 8 * col) % 128
    pick = jnp.where(sr == 2 * want_b + sc // 128, 1.0, 0.0).astype(BF16)

    def prep(a, carry):
        block = lad_ref[pl.ds(pl.multiple_of(a * 240, 240), 240), :]
        got = lax.dot_general(block, pick, (((0,), (0,)), ((), ())), preferred_element_type=F32)
        ab = jnp.bitwise_xor(irr_b, irr_of(row * NA + a))
        both = []
        for c in range(2):
            keep = jnp.bitwise_xor(ab, irr_c[c]) == irr_d
            both.append(jnp.where(keep, got[:, c * 128:(c + 1) * 128], 0.0))
        lt[x, a] = jnp.concatenate(both, axis=0).astype(BF16)
        return carry

    pl.semaphore_wait(barrier, 8 + 6 - jnp.where(jnp.logical_and(xt == x, core == 0), 1, 0))

    def s1_plane(n):
        even = jnp.where(n == 0, 6, jnp.where(n == 1, 8, jnp.where(n == 2, 4, jnp.where(n == 3, 10, jnp.where(n == 4, 2, 0)))))
        odd = jnp.where(n == 0, 5, jnp.where(n == 1, 7, jnp.where(n == 2, 3, jnp.where(n == 3, 9, jnp.where(n == 4, 1, 11)))))
        return (z + jnp.where(core == 0, even, odd)) % 12

    def s1_copy(n):
        zz = s1_plane(n)
        return pltpu.make_async_remote_copy(
            src_ref=shard, dst_ref=sh_all.at[s_mine, ip_mine, x],
            send_sem=s1_send.at[n], recv_sem=s1_recv.at[ip_mine, x],
            device_id=dev(zz, y, col, xt), device_id_type=MESH,
        )

    def s1_here(n):
        return jnp.logical_and(s1_plane(n) == z, xt == x)

    stays = jnp.logical_and(xt == x, core == 0)

    def s1_go(n, carry):
        @pl.when(jnp.logical_not(s1_here(n)))
        def _():
            s1_copy(n).start()

        return carry

    lax.fori_loop(0, 6, s1_go, 0)

    @pl.when(stays)
    def _():
        pltpu.make_async_copy(shard, sh_all.at[s_mine, ip_mine, x], own_sem).start()

    def x_own(j, side):
        return pltpu.make_async_remote_copy(
            src_ref=lt.at[x, pl.ds(2 * j, 2)], dst_ref=lt.at[x, pl.ds(2 * j, 2)],
            send_sem=x_send.at[side, j], recv_sem=x_recv.at[side, j],
            device_id=dev(z, y, col, left if side == 0 else right), device_id_type=MESH,
        )

    def x_fwd(j, side):
        owner = right if side == 0 else left
        a = 2 * j + (1 if side == 0 else 0)
        return pltpu.make_async_remote_copy(
            src_ref=lt.at[owner, a], dst_ref=lt.at[owner, a],
            send_sem=x_send.at[2 + side, j], recv_sem=x_recv.at[2 + side, j],
            device_id=dev(z, y, col, left if side == 0 else right), device_id_type=MESH,
        )

    loads[4].wait()
    for j in range(CH):
        lax.fori_loop(2 * j, 2 * j + 2, prep, 0)
        if j < 3:
            x_own(j, 0).start()
            x_own(j, 1).start()

    a_f[...] = jnp.zeros_like(a_f)
    of[NA * 256:, :] = jnp.zeros((6 * 256, 128), F32)
    pi = lax.broadcasted_iota(jnp.int32, (128, 128), 0)
    pj = lax.broadcasted_iota(jnp.int32, (128, 128), 1)
    occ_row = vec_f[1:2, 0:128]
    def occ_i_of(half):
        return jnp.sum(jnp.where(pj == (2 * half + pi // 64) * 4 + x, occ_row, 0.0), axis=1, keepdims=True)

    occ_k = jnp.sum(jnp.where(pj == pi % 64, occ_row, 0.0), axis=1, keepdims=True)
    occ_half = [occ_i_of(1 - yh) + occ_k, occ_i_of(yh) + occ_k]


    cyc_copy.wait()
    lane3 = lax.broadcasted_iota(jnp.int32, (1, 1, 128), 2)
    for t in range(4):
        @pl.when(col == t)
        def _():
            def rot(m, carry):
                lo = max(t - 1, 0) * 128
                for u in range(2):
                    k = 2 * m + u
                    if t < 3:
                        here = cyc[pl.ds(k, 1), :, t * 128:(t + 1) * 128]
                    else:
                        here = jnp.concatenate(
                            [cyc[pl.ds(k, 1), :, 384:480], cyc[pl.ds(k, 1), :, 352:384]], axis=2
                        )
                    there = cyc[pl.ds(k, 1), :, lo:lo + 128]
                    crot[pl.ds(m, 1), :, u * 128:(u + 1) * 128] = jnp.where(lane3 < 120 - 8 * t, here, there)
                return carry

            lax.fori_loop(0, NK // 2, rot, 0)

    def unit(s, h, mine):
        half = (1 - yh) if h == 0 else yh
        share = parity(s) if mine else 1 - parity(s)
        return sh_all.at[s, 2 * half + share]

    def s2_copy(t, h):
        return pltpu.make_async_remote_copy(
            src_ref=unit(s_here, h, True), dst_ref=unit(s_here, h, True),
            send_sem=s2_send.at[t - 1, h], recv_sem=s2_recv.at[s_here, h],
            device_id=dev(z, (y + t) % 4, col, x), device_id_type=MESH,
        )

    def s2_wait(s, h):
        return pltpu.make_async_remote_copy(
            src_ref=unit(s, h, True), dst_ref=unit(s, h, True),
            send_sem=s2_send.at[0, h], recv_sem=s2_recv.at[s, h],
            device_id=dev(z, (y + 1) % 4, col, x), device_id_type=MESH,
        )

    other = 2 * yh + 1 - core

    def sib_copy(s, h):
        return pltpu.make_async_remote_copy(
            src_ref=unit(s, h, True), dst_ref=unit(s, h, True),
            send_sem=b_send.at[s, h], recv_sem=b_recv.at[s, h],
            device_id=dev(z, y, other, x), device_id_type=MESH,
        )

    def sib_wait(s, h):
        return pltpu.make_async_remote_copy(
            src_ref=unit(s, h, False), dst_ref=unit(s, h, False),
            send_sem=b_send.at[s, h], recv_sem=b_recv.at[s, h],
            device_id=dev(z, y, other, x), device_id_type=MESH,
        )

    def forward(j):
        x_own(j, 0).wait_recv()
        x_own(j, 1).wait_recv()
        x_fwd(j, 0).start()
        x_fwd(j, 1).start()
        if j + 3 < CH:
            x_own(j + 3, 0).start()
            x_own(j + 3, 1).start()

    forward(0)

    @pl.when(stays)
    def _():
        pltpu.make_async_copy(shard, sh_all.at[s_mine, ip_mine, x], own_sem).wait()

    @pl.when(relay)
    def _():
        for h in range(2):
            half = (1 - yh) if h == 0 else yh
            i4 = 2 * half + parity(s_here)
            zz = 3 * i4 + z_off

            def got(xx, carry):
                @pl.when(jnp.logical_or(zz != z, xx != x))
                def _():
                    pltpu.make_async_remote_copy(
                        src_ref=shard, dst_ref=sh_all.at[s_here, i4, xx],
                        send_sem=s1_send.at[0], recv_sem=s1_recv.at[i4, xx],
                        device_id=dev(z, y, other, x), device_id_type=MESH,
                    ).wait_recv()

                return carry

            lax.fori_loop(0, 4, got, 0)
            for t in (2, 1, 3):
                s2_copy(t, h).start()
            sib_copy(s_here, h).start()

    def pass_on(h):
        for s in range(3):
            @pl.when(s_here != s)
            def _():
                s2_wait(s, h).wait_recv()
                sib_copy(s, h).start()

    def operand(h):
        half = (1 - yh) if h == 0 else yh
        for s in range(3):
            sib_wait(s, h).wait_recv()
        base = pl.multiple_of(half * 128, 128)
        for xx in range(4):
            for n in range(2):
                for s in range(3):
                    got = sh_all[s, 2 * half + n, xx].astype(F32)
                    top = n * 64 + s * 20
                    a_f[top:top + 20, 0:128] = got[0:20]
                    a_f[top:top + 20, 128:256] = got[24:44]
            a_b[xx, pl.ds(base, 128), :] = a_f[...].astype(BF16)

    forward(1)
    pass_on(0)
    operand(0)

    partners = [(2, 0), (2, 1), (0, 1)]

    def e_copy(p, j):
        dh, dc = partners[p]
        to = ((yh * 2 + dh) % 4) + (core + dc) % 2
        return pltpu.make_async_remote_copy(
            src_ref=nb.at[to, pl.ds(2 * j, 2)], dst_ref=rb.at[col, pl.ds(2 * j, 2)],
            send_sem=e_send.at[p, j], recv_sem=e_recv.at[p, j],
            device_id=dev(z, y, to, x), device_id_type=MESH,
        )

    def e_wait(p, j):
        dh, dc = partners[p]
        frm = ((yh * 2 + dh) % 4) + (core + dc) % 2
        pltpu.make_async_remote_copy(
            src_ref=nb.at[frm, pl.ds(2 * j, 2)], dst_ref=rb.at[frm, pl.ds(2 * j, 2)],
            send_sem=e_send.at[p, j], recv_sem=e_recv.at[p, j],
            device_id=dev(z, y, frm, x), device_id_type=MESH,
        ).wait_recv()

    def block(j, h):
        half = (1 - yh) if h == 0 else yh
        base = pl.multiple_of(half * 128, 128)
        total = None
        for xx in range(4):
            w = jnp.concatenate([lt[xx, 2 * j], lt[xx, 2 * j + 1]], axis=1)
            term = jnp.dot(a_b[xx, pl.ds(base, 128), 0:KD], w, preferred_element_type=F32)
            total = term if total is None else total + term
        occ = occ_half[h]
        for g in range(2):
            a = 2 * j + g
            denom = (ene_of(a) + ene_b) - occ
            new = (total[:, g * 128:(g + 1) * 128] / denom).astype(BF16)
            nb[2 * half, a] = new[0:64]
            nb[2 * half + 1, a] = new[64:128]
            of[pl.ds(pl.multiple_of(a * 256 + half * 128, 128), 128), :] = new.astype(F32)
        for p in ((0, 1) if h == 0 else (2,)):
            e_copy(p, j).start()

    def diag_in(j):
        x_fwd(j, 0).wait_recv()
        x_fwd(j, 1).wait_recv()

    diag_in(0)
    block(0, 0)
    forward(2)
    pass_on(1)
    diag_in(1)
    block(1, 0)
    forward(3)
    operand(1)
    block(0, 1)
    block(1, 1)
    diag_in(2)
    block(2, 0)
    block(2, 1)
    forward(4)
    for j in range(3, CH):
        diag_in(j)
        block(j, 0)
        block(j, 1)

    rb[pl.ds(col, 1)] = nb[pl.ds(col, 1)]

    def cycle(m, acc):
        parts = []
        for u in range(2):
            rows = [of[pl.ds(i4 * 64 + 2 * m + u, 16, stride=256), :] for i4 in range(4)]
            parts.append(jnp.concatenate(rows, axis=0).astype(BF16))
        left_op = jnp.concatenate(parts, axis=1)
        return acc + lax.dot_general(left_op, crot[m], (((1,), (1,)), ((), ())), preferred_element_type=F32)

    zsum = lax.fori_loop(0, NK // 2, cycle, jnp.zeros((64, NQ), F32), unroll=5)
    zw = jnp.concatenate([zsum, jnp.zeros((64, 64), F32)], axis=1)
    for i4 in range(4):
        zp[i4] = zw[i4 * 16:(i4 + 1) * 16]
    zr[pl.ds(col, 1)] = zp[pl.ds(col, 1)]

    def z_copy(p):
        dh, dc = partners[p]
        to = ((yh * 2 + dh) % 4) + (core + dc) % 2
        return pltpu.make_async_remote_copy(
            src_ref=zp.at[to], dst_ref=zr.at[col],
            send_sem=z_send.at[p], recv_sem=z_recv.at[p],
            device_id=dev(z, y, to, x), device_id_type=MESH,
        )

    def z_wait(p):
        dh, dc = partners[p]
        frm = ((yh * 2 + dh) % 4) + (core + dc) % 2
        pltpu.make_async_remote_copy(
            src_ref=zp.at[frm], dst_ref=zr.at[frm],
            send_sem=z_send.at[p], recv_sem=z_recv.at[p],
            device_id=dev(z, y, frm, x), device_id_type=MESH,
        ).wait_recv()

    for p in range(3):
        z_copy(p).start()

    def out_copy(j):
        part = pl.ds(2 * j, 2)
        return pltpu.make_async_copy(out_ref.at[part], out_hbm.at[part], out_sem.at[j])

    z_out = pltpu.make_async_copy(z_ref, z_hbm, out_sem.at[CH])

    lane_o = lax.broadcasted_iota(jnp.int32, (1, 128), 1)
    for j in range(CH):
        for p in range(3):
            e_wait(p, j)
        for h in range(2):
            a = 2 * j + h
            for t in range(3):
                tile = jnp.where(lane_o < 120 - 8 * t, rb[t, a], rb[t + 1, a])
                out_ref[a, :, t * 128:(t + 1) * 128] = tile[:NK]
            out_ref[a, :, 384:480] = rb[3, a][:NK, :96]
        out_copy(j).start()

    for p in range(3):
        z_wait(p)
    zt = (zr[0] + zr[1]) + (zr[2] + zr[3])
    z_ref[:, 0, :] = zt[:NA, :NQ]
    z_out.start()

    def s1_done(n, carry):
        @pl.when(jnp.logical_not(s1_here(n)))
        def _():
            s1_copy(n).wait_send()

        return carry

    lax.fori_loop(0, 6, s1_done, 0)

    @pl.when(relay)
    def _():
        for h in range(2):
            for t in range(1, 4):
                s2_copy(t, h).wait_send()

    for h in range(2):
        for s in range(3):
            sib_copy(s, h).wait_send()

    for j in range(CH):
        for side in range(2):
            x_own(j, side).wait_send()
            x_fwd(j, side).wait_send()
        for p in range(3):
            e_copy(p, j).wait_send()
    for p in range(3):
        z_copy(p).wait_send()
    for j in range(CH):
        out_copy(j).wait()
    z_out.wait()


def hand_on(amps_in, cyc_in, amps_out, cyc_out, amps, cyc, sem_in, sem_out):
    refs = [(amps_in.at[pl.ds(2 * j, 2)], amps.at[pl.ds(2 * j, 2)], amps_out.at[pl.ds(2 * j, 2)]) for j in range(CH)]
    refs.append((cyc_in, cyc, cyc_out))
    reads = [pltpu.make_async_copy(src, mid, sem_in.at[n]) for n, (src, mid, _) in enumerate(refs)]
    writes = [pltpu.make_async_copy(mid, dst, sem_out.at[n]) for n, (_, mid, dst) in enumerate(refs)]
    for copy in reads:
        copy.start()
    for read, write in zip(reads, writes):
        read.wait()
        write.start()
    for copy in writes:
        copy.wait()


def on_device(amp_old, ladder_int, cycle_int, virt_irrep, occ_energy, virt_energy):
    hbm = pl.BlockSpec(memory_space=pltpu.HBM)
    dma = pltpu.SemaphoreType.DMA
    lad = ladder_int.reshape(2 * NA * NB_, ND)
    out_shape = (
        jax.ShapeDtypeStruct((NA, NK, 480), BF16),
        jax.ShapeDtypeStruct((NA, 1, NQ), F32),
    )
    amps, cyc = pl.pallas_call(
        kernel,
        name="ladder",
        out_shape=out_shape,
        in_specs=[hbm] * 6,
        out_specs=(hbm, hbm),
        scratch_shapes=[
            pltpu.VMEM((NA, NK, 480), BF16),
            pltpu.VMEM((NA, 1, NQ), F32),
            pltpu.VMEM((20, 2, ND), BF16),
            pltpu.VMEM((2 * NA * NB_, ND), BF16),
            pltpu.VMEM((1, 480), jnp.int32),
            pltpu.VMEM((1, NK), F32),
            pltpu.VMEM((1, 480), F32),
            pltpu.VMEM((8, 512), F32),
            pltpu.VMEM((8, 512), jnp.int32),
            pltpu.VMEM((48, 128), BF16),
            pltpu.VMEM((3, 4, 4, 48, 128), BF16),
            pltpu.VMEM((4, NA, KD, 128), BF16),
            pltpu.VMEM((128, 256), F32),
            pltpu.VMEM((4, 256, 256), BF16),
            pltpu.VMEM((4, NA, 64, 128), BF16),
            pltpu.VMEM((4, NA, 64, 128), BF16),
            pltpu.VMEM((16 * 256, 128), F32),
            pltpu.VMEM((NK, NQ, 480), BF16),
            pltpu.VMEM((NK // 2, NQ, 256), BF16),
            pltpu.VMEM((4, 16, 128), F32),
            pltpu.VMEM((4, 16, 128), F32),
            dma((6,)), dma((6,)), dma, dma((6,)), dma((4, 4)), dma((3, 2)), dma((3, 2)), dma((3, 2)), dma((3, 2)),
            dma((4, CH)), dma((4, CH)), dma((3, CH)), dma((3, CH)), dma((3,)), dma((3,)),
        ],
        compiler_params=pltpu.CompilerParams(
            collective_id=0, has_side_effects=True, vmem_limit_bytes=60 << 20
        ),
    )(
        amp_old, lad, cycle_int,
        virt_irrep.reshape(1, 480), occ_energy.reshape(1, 60), virt_energy.reshape(1, 480),
    )
    amps, cyc = pl.pallas_call(
        hand_on,
        name="hand_on",
        out_shape=out_shape,
        in_specs=[hbm, hbm],
        out_specs=(hbm, hbm),
        scratch_shapes=[
            pltpu.VMEM((NA, NK, 480), BF16),
            pltpu.VMEM((NA, 1, NQ), F32),
            dma((CH + 1,)), dma((CH + 1,)),
        ],
        compiler_params=pltpu.CompilerParams(vmem_limit_bytes=60 << 20),
    )(amps, cyc)
    return amps.transpose(1, 0, 2)[None], cyc.transpose(1, 0, 2)


def solution(mesh):
    placed = (P("row", None, "dep"), P("row", "col", None, "dep"), P(), P(), P(), P())
    return jax.shard_map(
        on_device,
        mesh=mesh,
        in_specs=placed,
        out_specs=(P(("col", "dep"), None, "row", None), P(("col", "dep"), "row", None)),
        check_vma=False,
    )
```

```python
import jax
import jax.numpy as jnp
from jax import lax
from jax.experimental import pallas as pl
from jax.experimental.pallas import tpu as pltpu
from jax.sharding import PartitionSpec as P

MESH = pl.DeviceIdType.MESH
F32 = jnp.float32
BF16 = jnp.bfloat16
NX, NY, NZ = 4, 4, 12
NA, NB_, ND, NK, NQ = 10, 120, 120, 60, 64
CH = 5
KD = 2 * ND


def kernel(
    amp_hbm, lad_hbm, cyc_hbm, irr_hbm, occ_hbm, ene_hbm,
    out_hbm, z_hbm,
    out_ref, z_ref, amp_ref, lad_ref, irr_ref, occ_ref, ene_ref, vec_f, vec_i, shard, sh_all, lt, a_f, a_b, nb, rb, of, cyc, crot, zp, zr,
    in_sem, out_sem, own_sem, s1_send, s1_recv, s2_send, s2_recv, b_send, b_recv, x_send, x_recv, e_send, e_recv, z_send, z_recv,
):
    row = lax.axis_index("row")
    col = lax.axis_index("col")
    x = lax.axis_index("dep")
    z = row // 4
    y = row % 4
    yh = col // 2
    core = col % 2

    def dev(zz, yy, cc, xx):
        return (zz * 4 + yy, cc, xx)

    r12 = 4 * (z % 3) + y
    xt = r12 // 3
    s_mine = r12 % 3
    ip_mine = z // 3
    s_here = (x + y) % 4
    z_off = (3 * x + s_here) // 4
    relay = s_here < 3

    left = (x + 3) % 4
    right = (x + 1) % 4
    diag = (x + 2) % 4

    loads = [
        pltpu.make_async_copy(src, dst, in_sem.at[n])
        for n, (src, dst) in enumerate(
            [(amp_hbm, amp_ref), (irr_hbm, irr_ref), (occ_hbm, occ_ref), (ene_hbm, ene_ref), (lad_hbm, lad_ref), (cyc_hbm, cyc)]
        )
    ]
    for copy in loads:
        copy.start()
    cyc_copy = loads[5]
    barrier = pltpu.get_barrier_semaphore()

    def parity(s):
        return (core + (3 * x + s) // 4 + z) % 2

    def signal(d):
        pl.semaphore_signal(barrier, inc=1, device_id=d, device_id_type=MESH)

    @pl.when(relay)
    def _():
        def go(n, carry):
            zz = 3 * (2 * (n // 4) + parity(s_here)) + z_off
            xx = n % 4

            @pl.when(jnp.logical_or(zz != z, xx != x))
            def _():
                signal(dev(zz, y, col, xx))

            return carry

        lax.fori_loop(0, 8, go, 0)

    for t in range(1, 4):
        signal(dev(z, (y + t) % 4, col, x))
    signal(dev(z, y, col, left))
    signal(dev(z, y, col, right))
    for t in range(1, 4):
        signal(dev(z, y, (col + t) % 4, x))

    loads[0].wait()

    raw = amp_ref[...]
    wide = jnp.concatenate(
        [raw[:, 0, :].astype(F32), raw[:, 1, :].astype(F32), jnp.zeros((20, 16), F32)], axis=1
    )
    gap = jnp.zeros((4, 128), F32)
    shard[...] = jnp.concatenate([wide[:, :128], gap, wide[:, 128:], gap], axis=0).astype(BF16)

    pl.semaphore_wait(barrier, 8 + 6 - jnp.where(jnp.logical_and(xt == x, core == 0), 1, 0))

    def s1_plane(n):
        even = jnp.where(n == 0, 6, jnp.where(n == 1, 8, jnp.where(n == 2, 4, jnp.where(n == 3, 10, jnp.where(n == 4, 2, 0)))))
        odd = jnp.where(n == 0, 5, jnp.where(n == 1, 7, jnp.where(n == 2, 3, jnp.where(n == 3, 9, jnp.where(n == 4, 1, 11)))))
        return (z + jnp.where(core == 0, even, odd)) % 12

    def s1_copy(n):
        zz = s1_plane(n)
        return pltpu.make_async_remote_copy(
            src_ref=shard, dst_ref=sh_all.at[s_mine, ip_mine, x],
            send_sem=s1_send.at[n], recv_sem=s1_recv.at[ip_mine, x],
            device_id=dev(zz, y, col, xt), device_id_type=MESH,
        )

    def s1_here(n):
        return jnp.logical_and(s1_plane(n) == z, xt == x)

    stays = jnp.logical_and(xt == x, core == 0)

    def s1_go(n, carry):
        @pl.when(jnp.logical_not(s1_here(n)))
        def _():
            s1_copy(n).start()

        return carry

    lax.fori_loop(0, 6, s1_go, 0)

    @pl.when(stays)
    def _():
        pltpu.make_async_copy(shard, sh_all.at[s_mine, ip_mine, x], own_sem).start()

    for copy in loads[1:4]:
        copy.wait()

    vec_f[...] = jnp.zeros_like(vec_f)
    vec_i[...] = jnp.zeros_like(vec_i)
    vec_f[0:1, 0:480] = ene_ref[...]
    vec_f[1:2, 0:60] = occ_ref[...]
    vec_i[0:1, 0:480] = irr_ref[...]
    lane = lax.broadcasted_iota(jnp.int32, (1, 128), 1)
    edge = 120 - 8 * col
    prev = jnp.maximum(col - 1, 0)
    at = pl.multiple_of(col * 128, 128)
    before = pl.multiple_of(prev * 128, 128)
    ene_b = jnp.where(lane < edge, vec_f[0:1, pl.ds(at, 128)], vec_f[0:1, pl.ds(before, 128)])
    irr_b = jnp.where(lane < edge, vec_i[0:1, pl.ds(at, 128)], vec_i[0:1, pl.ds(before, 128)])
    ii = lax.broadcasted_iota(jnp.int32, (ND, 512), 0)
    jj = lax.broadcasted_iota(jnp.int32, (ND, 512), 1)
    irr_d = jnp.sum(jnp.where(jj == ii + ND * x, vec_i[0:1, :].astype(F32), 0.0), axis=1, keepdims=True).astype(jnp.int32)
    wide_lane = lax.broadcasted_iota(jnp.int32, (1, 512), 1)

    def ene_of(a):
        return jnp.sum(jnp.where(wide_lane == row * NA + a, vec_f[0:1, :], 0.0), axis=1, keepdims=True)

    def irr_of(n):
        picked = jnp.sum(jnp.where(wide_lane == n, vec_i[0:1, :].astype(F32), 0.0), axis=1, keepdims=True)
        return picked.astype(jnp.int32)

    irr_c = [irr_of(c) for c in range(2)]

    sr = lax.broadcasted_iota(jnp.int32, (2 * NB_, 256), 0)
    sc = lax.broadcasted_iota(jnp.int32, (2 * NB_, 256), 1)
    want_b = (sc % 128 + 8 * col) % 128
    pick = jnp.where(sr == 2 * want_b + sc // 128, 1.0, 0.0).astype(BF16)

    def prep(a, carry):
        block = lad_ref[pl.ds(pl.multiple_of(a * 240, 240), 240), :]
        got = lax.dot_general(block, pick, (((0,), (0,)), ((), ())), preferred_element_type=F32)
        ab = jnp.bitwise_xor(irr_b, irr_of(row * NA + a))
        both = []
        for c in range(2):
            keep = jnp.bitwise_xor(ab, irr_c[c]) == irr_d
            both.append(jnp.where(keep, got[:, c * 128:(c + 1) * 128], 0.0))
        lt[x, a] = jnp.concatenate(both, axis=0).astype(BF16)
        return carry

    def x_own(j, side):
        return pltpu.make_async_remote_copy(
            src_ref=lt.at[x, pl.ds(2 * j, 2)], dst_ref=lt.at[x, pl.ds(2 * j, 2)],
            send_sem=x_send.at[side, j], recv_sem=x_recv.at[side, j],
            device_id=dev(z, y, col, left if side == 0 else right), device_id_type=MESH,
        )

    def x_fwd(j, side):
        owner = right if side == 0 else left
        a = 2 * j + (1 if side == 0 else 0)
        return pltpu.make_async_remote_copy(
            src_ref=lt.at[owner, a], dst_ref=lt.at[owner, a],
            send_sem=x_send.at[2 + side, j], recv_sem=x_recv.at[2 + side, j],
            device_id=dev(z, y, col, left if side == 0 else right), device_id_type=MESH,
        )

    loads[4].wait()
    for j in range(CH):
        lax.fori_loop(2 * j, 2 * j + 2, prep, 0)
        if j < 3:
            x_own(j, 0).start()
            x_own(j, 1).start()

    a_f[...] = jnp.zeros_like(a_f)
    of[NA * 256:, :] = jnp.zeros((6 * 256, 128), F32)
    pi = lax.broadcasted_iota(jnp.int32, (128, 128), 0)
    pj = lax.broadcasted_iota(jnp.int32, (128, 128), 1)
    occ_row = vec_f[1:2, 0:128]
    def occ_i_of(half):
        return jnp.sum(jnp.where(pj == (2 * half + pi // 64) * 4 + x, occ_row, 0.0), axis=1, keepdims=True)

    occ_k = jnp.sum(jnp.where(pj == pi % 64, occ_row, 0.0), axis=1, keepdims=True)
    occ_half = [occ_i_of(1 - yh) + occ_k, occ_i_of(yh) + occ_k]


    cyc_copy.wait()
    lane3 = lax.broadcasted_iota(jnp.int32, (1, 1, 128), 2)
    for t in range(4):
        @pl.when(col == t)
        def _():
            def rot(m, carry):
                lo = max(t - 1, 0) * 128
                for u in range(2):
                    k = 2 * m + u
                    if t < 3:
                        here = cyc[pl.ds(k, 1), :, t * 128:(t + 1) * 128]
                    else:
                        here = jnp.concatenate(
                            [cyc[pl.ds(k, 1), :, 384:480], cyc[pl.ds(k, 1), :, 352:384]], axis=2
                        )
                    there = cyc[pl.ds(k, 1), :, lo:lo + 128]
                    crot[pl.ds(m, 1), :, u * 128:(u + 1) * 128] = jnp.where(lane3 < 120 - 8 * t, here, there)
                return carry

            lax.fori_loop(0, NK // 2, rot, 0)

    def unit(s, h, mine):
        half = (1 - yh) if h == 0 else yh
        share = parity(s) if mine else 1 - parity(s)
        return sh_all.at[s, 2 * half + share]

    def s2_copy(t, h):
        return pltpu.make_async_remote_copy(
            src_ref=unit(s_here, h, True), dst_ref=unit(s_here, h, True),
            send_sem=s2_send.at[t - 1, h], recv_sem=s2_recv.at[s_here, h],
            device_id=dev(z, (y + t) % 4, col, x), device_id_type=MESH,
        )

    def s2_wait(s, h):
        return pltpu.make_async_remote_copy(
            src_ref=unit(s, h, True), dst_ref=unit(s, h, True),
            send_sem=s2_send.at[0, h], recv_sem=s2_recv.at[s, h],
            device_id=dev(z, (y + 1) % 4, col, x), device_id_type=MESH,
        )

    other = 2 * yh + 1 - core

    def sib_copy(s, h):
        return pltpu.make_async_remote_copy(
            src_ref=unit(s, h, True), dst_ref=unit(s, h, True),
            send_sem=b_send.at[s, h], recv_sem=b_recv.at[s, h],
            device_id=dev(z, y, other, x), device_id_type=MESH,
        )

    def sib_wait(s, h):
        return pltpu.make_async_remote_copy(
            src_ref=unit(s, h, False), dst_ref=unit(s, h, False),
            send_sem=b_send.at[s, h], recv_sem=b_recv.at[s, h],
            device_id=dev(z, y, other, x), device_id_type=MESH,
        )

    def forward(j):
        x_own(j, 0).wait_recv()
        x_own(j, 1).wait_recv()
        x_fwd(j, 0).start()
        x_fwd(j, 1).start()
        if j + 3 < CH:
            x_own(j + 3, 0).start()
            x_own(j + 3, 1).start()

    forward(0)

    @pl.when(stays)
    def _():
        pltpu.make_async_copy(shard, sh_all.at[s_mine, ip_mine, x], own_sem).wait()

    @pl.when(relay)
    def _():
        for h in range(2):
            half = (1 - yh) if h == 0 else yh
            i4 = 2 * half + parity(s_here)
            zz = 3 * i4 + z_off

            def got(xx, carry):
                @pl.when(jnp.logical_or(zz != z, xx != x))
                def _():
                    pltpu.make_async_remote_copy(
                        src_ref=shard, dst_ref=sh_all.at[s_here, i4, xx],
                        send_sem=s1_send.at[0], recv_sem=s1_recv.at[i4, xx],
                        device_id=dev(z, y, other, x), device_id_type=MESH,
                    ).wait_recv()

                return carry

            lax.fori_loop(0, 4, got, 0)
            for t in (2, 1, 3):
                s2_copy(t, h).start()
            sib_copy(s_here, h).start()

    def pass_on(h):
        for s in range(3):
            @pl.when(s_here != s)
            def _():
                s2_wait(s, h).wait_recv()
                sib_copy(s, h).start()

    def operand(h):
        half = (1 - yh) if h == 0 else yh
        for s in range(3):
            sib_wait(s, h).wait_recv()
        base = pl.multiple_of(half * 128, 128)
        for xx in range(4):
            for n in range(2):
                for s in range(3):
                    got = sh_all[s, 2 * half + n, xx].astype(F32)
                    top = n * 64 + s * 20
                    a_f[top:top + 20, 0:128] = got[0:20]
                    a_f[top:top + 20, 128:256] = got[24:44]
            a_b[xx, pl.ds(base, 128), :] = a_f[...].astype(BF16)

    forward(1)
    forward(2)
    pass_on(0)
    operand(0)

    partners = [(2, 0), (2, 1), (0, 1)]

    def e_copy(p, j):
        dh, dc = partners[p]
        to = ((yh * 2 + dh) % 4) + (core + dc) % 2
        return pltpu.make_async_remote_copy(
            src_ref=nb.at[to, pl.ds(2 * j, 2)], dst_ref=rb.at[col, pl.ds(2 * j, 2)],
            send_sem=e_send.at[p, j], recv_sem=e_recv.at[p, j],
            device_id=dev(z, y, to, x), device_id_type=MESH,
        )

    def e_wait(p, j):
        dh, dc = partners[p]
        frm = ((yh * 2 + dh) % 4) + (core + dc) % 2
        pltpu.make_async_remote_copy(
            src_ref=nb.at[frm, pl.ds(2 * j, 2)], dst_ref=rb.at[frm, pl.ds(2 * j, 2)],
            send_sem=e_send.at[p, j], recv_sem=e_recv.at[p, j],
            device_id=dev(z, y, frm, x), device_id_type=MESH,
        ).wait_recv()

    def block(j, h):
        half = (1 - yh) if h == 0 else yh
        base = pl.multiple_of(half * 128, 128)
        total = None
        for xx in range(4):
            w = jnp.concatenate([lt[xx, 2 * j], lt[xx, 2 * j + 1]], axis=1)
            term = jnp.dot(a_b[xx, pl.ds(base, 128), 0:KD], w, preferred_element_type=F32)
            total = term if total is None else total + term
        occ = occ_half[h]
        for g in range(2):
            a = 2 * j + g
            denom = (ene_of(a) + ene_b) - occ
            new = (total[:, g * 128:(g + 1) * 128] / denom).astype(BF16)
            nb[2 * half, a] = new[0:64]
            nb[2 * half + 1, a] = new[64:128]
            of[pl.ds(pl.multiple_of(a * 256 + half * 128, 128), 128), :] = new.astype(F32)
        for p in ((0, 1) if h == 0 else (2,)):
            e_copy(p, j).start()

    def diag_in(j):
        x_fwd(j, 0).wait_recv()
        x_fwd(j, 1).wait_recv()

    def z_copy(p):
        dh, dc = partners[p]
        to = ((yh * 2 + dh) % 4) + (core + dc) % 2
        return pltpu.make_async_remote_copy(
            src_ref=zp.at[to], dst_ref=zr.at[col],
            send_sem=z_send.at[p], recv_sem=z_recv.at[p],
            device_id=dev(z, y, to, x), device_id_type=MESH,
        )

    def z_wait(p):
        dh, dc = partners[p]
        frm = ((yh * 2 + dh) % 4) + (core + dc) % 2
        pltpu.make_async_remote_copy(
            src_ref=zp.at[frm], dst_ref=zr.at[frm],
            send_sem=z_send.at[p], recv_sem=z_recv.at[p],
            device_id=dev(z, y, frm, x), device_id_type=MESH,
        ).wait_recv()

    def cycle(h):
        half = (1 - yh) if h == 0 else yh

        def step(m, acc):
            parts = []
            for u in range(2):
                rows = [of[pl.ds((2 * half + n) * 64 + 2 * m + u, 16, stride=256), :] for n in range(2)]
                parts.append(jnp.concatenate(rows, axis=0).astype(BF16))
            left_op = jnp.concatenate(parts, axis=1)
            return acc + lax.dot_general(left_op, crot[m], (((1,), (1,)), ((), ())), preferred_element_type=F32)

        zsum = lax.fori_loop(0, NK // 2, step, jnp.zeros((32, NQ), F32), unroll=6)
        zw = jnp.concatenate([zsum, jnp.zeros((32, 64), F32)], axis=1)
        for n in range(2):
            zp[2 * half + n] = zw[n * 16:(n + 1) * 16]
        for p in ((0, 1) if h == 0 else (2,)):
            z_copy(p).start()

    diag_in(0)
    block(0, 0)
    forward(3)
    pass_on(1)
    diag_in(1)
    block(1, 0)
    forward(4)
    diag_in(2)
    block(2, 0)
    operand(1)
    block(0, 1)
    diag_in(3)
    block(3, 0)
    block(1, 1)
    block(2, 1)
    diag_in(4)
    block(4, 0)
    cycle(0)
    block(3, 1)
    block(4, 1)
    cycle(1)
    rb[pl.ds(col, 1)] = nb[pl.ds(col, 1)]
    zr[pl.ds(col, 1)] = zp[pl.ds(col, 1)]

    def out_copy(j):
        part = pl.ds(2 * j, 2)
        return pltpu.make_async_copy(out_ref.at[part], out_hbm.at[part], out_sem.at[j])

    z_out = pltpu.make_async_copy(z_ref, z_hbm, out_sem.at[CH])

    lane_o = lax.broadcasted_iota(jnp.int32, (1, 128), 1)
    for j in range(CH):
        for p in range(3):
            e_wait(p, j)
        for h in range(2):
            a = 2 * j + h
            for t in range(3):
                tile = jnp.where(lane_o < 120 - 8 * t, rb[t, a], rb[t + 1, a])
                out_ref[a, :, t * 128:(t + 1) * 128] = tile[:NK]
            out_ref[a, :, 384:480] = rb[3, a][:NK, :96]
        out_copy(j).start()

    for p in range(3):
        z_wait(p)
    zt = (zr[0] + zr[1]) + (zr[2] + zr[3])
    z_ref[:, 0, :] = zt[:NA, :NQ]
    z_out.start()

    def s1_done(n, carry):
        @pl.when(jnp.logical_not(s1_here(n)))
        def _():
            s1_copy(n).wait_send()

        return carry

    lax.fori_loop(0, 6, s1_done, 0)

    @pl.when(relay)
    def _():
        for h in range(2):
            for t in range(1, 4):
                s2_copy(t, h).wait_send()

    for h in range(2):
        for s in range(3):
            sib_copy(s, h).wait_send()

    for j in range(CH):
        for side in range(2):
            x_own(j, side).wait_send()
            x_fwd(j, side).wait_send()
        for p in range(3):
            e_copy(p, j).wait_send()
    for p in range(3):
        z_copy(p).wait_send()
    for j in range(CH):
        out_copy(j).wait()
    z_out.wait()


def hand_on(amps_in, cyc_in, amps_out, cyc_out, amps, cyc, sem_in, sem_out):
    refs = [(amps_in.at[pl.ds(2 * j, 2)], amps.at[pl.ds(2 * j, 2)], amps_out.at[pl.ds(2 * j, 2)]) for j in range(CH)]
    refs.append((cyc_in, cyc, cyc_out))
    reads = [pltpu.make_async_copy(src, mid, sem_in.at[n]) for n, (src, mid, _) in enumerate(refs)]
    writes = [pltpu.make_async_copy(mid, dst, sem_out.at[n]) for n, (_, mid, dst) in enumerate(refs)]
    for copy in reads:
        copy.start()
    for read, write in zip(reads, writes):
        read.wait()
        write.start()
    for copy in writes:
        copy.wait()


def on_device(amp_old, ladder_int, cycle_int, virt_irrep, occ_energy, virt_energy):
    hbm = pl.BlockSpec(memory_space=pltpu.HBM)
    dma = pltpu.SemaphoreType.DMA
    lad = ladder_int.reshape(2 * NA * NB_, ND)
    out_shape = (
        jax.ShapeDtypeStruct((NA, NK, 480), BF16),
        jax.ShapeDtypeStruct((NA, 1, NQ), F32),
    )
    amps, cyc = pl.pallas_call(
        kernel,
        name="ladder",
        out_shape=out_shape,
        in_specs=[hbm] * 6,
        out_specs=(hbm, hbm),
        scratch_shapes=[
            pltpu.VMEM((NA, NK, 480), BF16),
            pltpu.VMEM((NA, 1, NQ), F32),
            pltpu.VMEM((20, 2, ND), BF16),
            pltpu.VMEM((2 * NA * NB_, ND), BF16),
            pltpu.VMEM((1, 480), jnp.int32),
            pltpu.VMEM((1, NK), F32),
            pltpu.VMEM((1, 480), F32),
            pltpu.VMEM((8, 512), F32),
            pltpu.VMEM((8, 512), jnp.int32),
            pltpu.VMEM((48, 128), BF16),
            pltpu.VMEM((3, 4, 4, 48, 128), BF16),
            pltpu.VMEM((4, NA, KD, 128), BF16),
            pltpu.VMEM((128, 256), F32),
            pltpu.VMEM((4, 256, 256), BF16),
            pltpu.VMEM((4, NA, 64, 128), BF16),
            pltpu.VMEM((4, NA, 64, 128), BF16),
            pltpu.VMEM((16 * 256, 128), F32),
            pltpu.VMEM((NK, NQ, 480), BF16),
            pltpu.VMEM((NK // 2, NQ, 256), BF16),
            pltpu.VMEM((4, 16, 128), F32),
            pltpu.VMEM((4, 16, 128), F32),
            dma((6,)), dma((6,)), dma, dma((6,)), dma((4, 4)), dma((3, 2)), dma((3, 2)), dma((3, 2)), dma((3, 2)),
            dma((4, CH)), dma((4, CH)), dma((3, CH)), dma((3, CH)), dma((3,)), dma((3,)),
        ],
        compiler_params=pltpu.CompilerParams(
            collective_id=0, has_side_effects=True, vmem_limit_bytes=60 << 20
        ),
    )(
        amp_old, lad, cycle_int,
        virt_irrep.reshape(1, 480), occ_energy.reshape(1, 60), virt_energy.reshape(1, 480),
    )
    amps, cyc = pl.pallas_call(
        hand_on,
        name="hand_on",
        out_shape=out_shape,
        in_specs=[hbm, hbm],
        out_specs=(hbm, hbm),
        scratch_shapes=[
            pltpu.VMEM((NA, NK, 480), BF16),
            pltpu.VMEM((NA, 1, NQ), F32),
            dma((CH + 1,)), dma((CH + 1,)),
        ],
        compiler_params=pltpu.CompilerParams(vmem_limit_bytes=60 << 20),
    )(amps, cyc)
    return amps.transpose(1, 0, 2)[None], cyc.transpose(1, 0, 2)


def solution(mesh):
    placed = (P("row", None, "dep"), P("row", "col", None, "dep"), P(), P(), P(), P())
    return jax.shard_map(
        on_device,
        mesh=mesh,
        in_specs=placed,
        out_specs=(P(("col", "dep"), None, "row", None), P(("col", "dep"), "row", None)),
        check_vma=False,
    )
```

```python
import jax
import jax.numpy as jnp
from jax import lax
from jax.experimental import pallas as pl
from jax.experimental.pallas import tpu as pltpu
from jax.sharding import PartitionSpec as P

MESH = pl.DeviceIdType.MESH
F32 = jnp.float32
BF16 = jnp.bfloat16
NX, NY, NZ = 4, 4, 12
NA, NB_, ND, NK, NQ = 10, 120, 120, 60, 64
CH = 5
KD = 2 * ND


def kernel(
    amp_hbm, lad_hbm, cyc_hbm, irr_hbm, occ_hbm, ene_hbm,
    out_hbm, z_hbm,
    out_ref, z_ref, pick_ref, amp_ref, lad_ref, irr_ref, occ_ref, ene_ref, vec_f, vec_i, shard, sh_all, lt, a_f, a_b, nb, rb, of, cyc, crot, zp, zr,
    in_sem, out_sem, own_sem, s1_send, s1_recv, s2_send, s2_recv, b_send, b_recv, x_send, x_recv, e_send, e_recv, z_send, z_recv,
):
    row = lax.axis_index("row")
    col = lax.axis_index("col")
    x = lax.axis_index("dep")
    z = row // 4
    y = row % 4
    yh = col // 2
    core = col % 2

    def dev(zz, yy, cc, xx):
        return (zz * 4 + yy, cc, xx)

    r12 = 4 * (z % 3) + y
    xt = r12 // 3
    s_mine = r12 % 3
    ip_mine = z // 3
    s_here = (x + y) % 4
    z_off = (3 * x + s_here) // 4
    relay = s_here < 3

    left = (x + 3) % 4
    right = (x + 1) % 4
    diag = (x + 2) % 4

    def pick_matrix():
        sr = lax.broadcasted_iota(jnp.int32, (2 * NB_, 256), 0)
        sc = lax.broadcasted_iota(jnp.int32, (2 * NB_, 256), 1)
        want_b = (sc % 128 + 8 * col) % 128
        return jnp.where(sr == 2 * want_b + sc // 128, 1.0, 0.0).astype(BF16)

    loads = [
        pltpu.make_async_copy(src, dst, in_sem.at[n])
        for n, (src, dst) in enumerate(
            [(amp_hbm, amp_ref), (lad_hbm, lad_ref), (irr_hbm, irr_ref), (occ_hbm, occ_ref), (ene_hbm, ene_ref), (cyc_hbm, cyc)]
        )
    ]
    for copy in loads[:5]:
        copy.start()
    cyc_copy = loads[5]
    barrier = pltpu.get_barrier_semaphore()

    def parity(s):
        return (core + (3 * x + s) // 4 + z) % 2

    def signal(d):
        pl.semaphore_signal(barrier, inc=1, device_id=d, device_id_type=MESH)

    @pl.when(relay)
    def _():
        def go(n, carry):
            zz = 3 * (2 * (n // 4) + parity(s_here)) + z_off
            xx = n % 4

            @pl.when(jnp.logical_or(zz != z, xx != x))
            def _():
                signal(dev(zz, y, col, xx))

            return carry

        lax.fori_loop(0, 8, go, 0)

    for t in range(1, 4):
        signal(dev(z, (y + t) % 4, col, x))
    signal(dev(z, y, col, left))
    signal(dev(z, y, col, right))
    for t in range(1, 4):
        signal(dev(z, y, (col + t) % 4, x))

    pick_ref[...] = pick_matrix()
    loads[0].wait()

    raw = amp_ref[...]
    wide = jnp.concatenate(
        [raw[:, 0, :].astype(F32), raw[:, 1, :].astype(F32), jnp.zeros((20, 16), F32)], axis=1
    )
    gap = jnp.zeros((4, 128), F32)
    shard[...] = jnp.concatenate([wide[:, :128], gap, wide[:, 128:], gap], axis=0).astype(BF16)

    pl.semaphore_wait(barrier, 8 + 6 - jnp.where(jnp.logical_and(xt == x, core == 0), 1, 0))

    def s1_plane(n):
        even = (6, 8, 4, 10, 2, 0)[n]
        odd = (5, 7, 3, 9, 1, 11)[n]
        return (z + jnp.where(core == 0, even, odd)) % 12

    def s1_copy(n):
        zz = s1_plane(n)
        return pltpu.make_async_remote_copy(
            src_ref=shard, dst_ref=sh_all.at[s_mine, ip_mine, x],
            send_sem=s1_send.at[n], recv_sem=s1_recv.at[ip_mine, x],
            device_id=dev(zz, y, col, xt), device_id_type=MESH,
        )

    def s1_here(n):
        return jnp.logical_and(s1_plane(n) == z, xt == x)

    stays = jnp.logical_and(xt == x, core == 0)

    def s1_go(n, carry):
        @pl.when(jnp.logical_not(s1_here(n)))
        def _():
            s1_copy(n).start()

        return carry

    for n in range(6):
        s1_go(n, 0)

    @pl.when(stays)
    def _():
        pltpu.make_async_copy(shard, sh_all.at[s_mine, ip_mine, x], own_sem).start()

    for copy in loads[2:5]:
        copy.wait()

    vec_f[...] = jnp.zeros_like(vec_f)
    vec_i[...] = jnp.zeros_like(vec_i)
    vec_f[0:1, 0:480] = ene_ref[...]
    vec_f[1:2, 0:60] = occ_ref[...]
    vec_i[0:1, 0:480] = irr_ref[...]
    lane = lax.broadcasted_iota(jnp.int32, (1, 128), 1)
    edge = 120 - 8 * col
    prev = jnp.maximum(col - 1, 0)
    at = pl.multiple_of(col * 128, 128)
    before = pl.multiple_of(prev * 128, 128)
    ene_b = jnp.where(lane < edge, vec_f[0:1, pl.ds(at, 128)], vec_f[0:1, pl.ds(before, 128)])
    irr_b = jnp.where(lane < edge, vec_i[0:1, pl.ds(at, 128)], vec_i[0:1, pl.ds(before, 128)])
    ii = lax.broadcasted_iota(jnp.int32, (ND, 512), 0)
    jj = lax.broadcasted_iota(jnp.int32, (ND, 512), 1)
    irr_d = jnp.sum(jnp.where(jj == ii + ND * x, vec_i[0:1, :].astype(F32), 0.0), axis=1, keepdims=True).astype(jnp.int32)
    wide_lane = lax.broadcasted_iota(jnp.int32, (1, 512), 1)

    def ene_of(a):
        return jnp.sum(jnp.where(wide_lane == row * NA + a, vec_f[0:1, :], 0.0), axis=1, keepdims=True)

    def irr_of(n):
        picked = jnp.sum(jnp.where(wide_lane == n, vec_i[0:1, :].astype(F32), 0.0), axis=1, keepdims=True)
        return picked.astype(jnp.int32)

    irr_c = [irr_of(c) for c in range(2)]

    def prep(a, carry):
        block = lad_ref[pl.ds(pl.multiple_of(a * 240, 240), 240), :]
        got = lax.dot_general(block, pick_ref[...], (((0,), (0,)), ((), ())), preferred_element_type=F32)
        ab = jnp.bitwise_xor(irr_b, irr_of(row * NA + a))
        both = []
        for c in range(2):
            keep = jnp.bitwise_xor(ab, irr_c[c]) == irr_d
            both.append(jnp.where(keep, got[:, c * 128:(c + 1) * 128], 0.0))
        lt[x, a] = jnp.concatenate(both, axis=0).astype(BF16)
        return carry

    def x_own(j, side):
        return pltpu.make_async_remote_copy(
            src_ref=lt.at[x, pl.ds(2 * j, 2)], dst_ref=lt.at[x, pl.ds(2 * j, 2)],
            send_sem=x_send.at[side, j], recv_sem=x_recv.at[side, j],
            device_id=dev(z, y, col, left if side == 0 else right), device_id_type=MESH,
        )

    def x_fwd(j, side):
        owner = right if side == 0 else left
        a = 2 * j + (1 if side == 0 else 0)
        return pltpu.make_async_remote_copy(
            src_ref=lt.at[owner, a], dst_ref=lt.at[owner, a],
            send_sem=x_send.at[2 + side, j], recv_sem=x_recv.at[2 + side, j],
            device_id=dev(z, y, col, left if side == 0 else right), device_id_type=MESH,
        )

    cyc_copy.start()
    loads[1].wait()
    for j in range(CH):
        lax.fori_loop(2 * j, 2 * j + 2, prep, 0)
        if j < 3:
            x_own(j, 0).start()
            x_own(j, 1).start()

    a_f[...] = jnp.zeros_like(a_f)
    of[NA * 256:, :] = jnp.zeros((6 * 256, 128), F32)
    pi = lax.broadcasted_iota(jnp.int32, (128, 128), 0)
    pj = lax.broadcasted_iota(jnp.int32, (128, 128), 1)
    occ_row = vec_f[1:2, 0:128]
    def occ_i_of(half):
        return jnp.sum(jnp.where(pj == (2 * half + pi // 64) * 4 + x, occ_row, 0.0), axis=1, keepdims=True)

    occ_k = jnp.sum(jnp.where(pj == pi % 64, occ_row, 0.0), axis=1, keepdims=True)
    occ_half = [occ_i_of(1 - yh) + occ_k, occ_i_of(yh) + occ_k]


    cyc_copy.wait()
    lane3 = lax.broadcasted_iota(jnp.int32, (1, 1, 128), 2)
    for t in range(4):
        @pl.when(col == t)
        def _():
            def rot(m, carry):
                lo = max(t - 1, 0) * 128
                for u in range(2):
                    k = 2 * m + u
                    if t < 3:
                        here = cyc[pl.ds(k, 1), :, t * 128:(t + 1) * 128]
                    else:
                        here = jnp.concatenate(
                            [cyc[pl.ds(k, 1), :, 384:480], cyc[pl.ds(k, 1), :, 352:384]], axis=2
                        )
                    there = cyc[pl.ds(k, 1), :, lo:lo + 128]
                    crot[pl.ds(m, 1), :, u * 128:(u + 1) * 128] = jnp.where(lane3 < 120 - 8 * t, here, there)
                return carry

            lax.fori_loop(0, NK // 2, rot, 0)

    def unit(s, h, mine):
        half = (1 - yh) if h == 0 else yh
        share = parity(s) if mine else 1 - parity(s)
        return sh_all.at[s, 2 * half + share]

    def s2_copy(t, h):
        return pltpu.make_async_remote_copy(
            src_ref=unit(s_here, h, True), dst_ref=unit(s_here, h, True),
            send_sem=s2_send.at[t - 1, h], recv_sem=s2_recv.at[s_here, h],
            device_id=dev(z, (y + t) % 4, col, x), device_id_type=MESH,
        )

    def s2_wait(s, h):
        return pltpu.make_async_remote_copy(
            src_ref=unit(s, h, True), dst_ref=unit(s, h, True),
            send_sem=s2_send.at[0, h], recv_sem=s2_recv.at[s, h],
            device_id=dev(z, (y + 1) % 4, col, x), device_id_type=MESH,
        )

    other = 2 * yh + 1 - core

    def sib_copy(s, h):
        return pltpu.make_async_remote_copy(
            src_ref=unit(s, h, True), dst_ref=unit(s, h, True),
            send_sem=b_send.at[s, h], recv_sem=b_recv.at[s, h],
            device_id=dev(z, y, other, x), device_id_type=MESH,
        )

    def sib_wait(s, h):
        return pltpu.make_async_remote_copy(
            src_ref=unit(s, h, False), dst_ref=unit(s, h, False),
            send_sem=b_send.at[s, h], recv_sem=b_recv.at[s, h],
            device_id=dev(z, y, other, x), device_id_type=MESH,
        )

    def forward(j):
        x_own(j, 0).wait_recv()
        x_own(j, 1).wait_recv()
        x_fwd(j, 0).start()
        x_fwd(j, 1).start()
        if j + 3 < CH:
            x_own(j + 3, 0).start()
            x_own(j + 3, 1).start()

    forward(0)

    @pl.when(stays)
    def _():
        pltpu.make_async_copy(shard, sh_all.at[s_mine, ip_mine, x], own_sem).wait()

    @pl.when(relay)
    def _():
        for h in range(2):
            half = (1 - yh) if h == 0 else yh
            i4 = 2 * half + parity(s_here)
            zz = 3 * i4 + z_off

            def got(xx, carry):
                @pl.when(jnp.logical_or(zz != z, xx != x))
                def _():
                    pltpu.make_async_remote_copy(
                        src_ref=shard, dst_ref=sh_all.at[s_here, i4, xx],
                        send_sem=s1_send.at[0], recv_sem=s1_recv.at[i4, xx],
                        device_id=dev(z, y, other, x), device_id_type=MESH,
                    ).wait_recv()

                return carry

            lax.fori_loop(0, 4, got, 0)
            for t in (2, 1, 3):
                s2_copy(t, h).start()
            sib_copy(s_here, h).start()

    def pass_on(h):
        for s in range(3):
            @pl.when(s_here != s)
            def _():
                s2_wait(s, h).wait_recv()
                sib_copy(s, h).start()

    def operand(h):
        half = (1 - yh) if h == 0 else yh
        for s in range(3):
            sib_wait(s, h).wait_recv()
        base = pl.multiple_of(half * 128, 128)
        for xx in range(4):
            for n in range(2):
                for s in range(3):
                    got = sh_all[s, 2 * half + n, xx].astype(F32)
                    top = n * 64 + s * 20
                    a_f[top:top + 20, 0:128] = got[0:20]
                    a_f[top:top + 20, 128:256] = got[24:44]
            a_b[xx, pl.ds(base, 128), :] = a_f[...].astype(BF16)

    forward(1)
    forward(2)
    pass_on(0)
    operand(0)

    partners = [(2, 0), (2, 1), (0, 1)]

    def e_copy(p, j):
        dh, dc = partners[p]
        to = ((yh * 2 + dh) % 4) + (core + dc) % 2
        return pltpu.make_async_remote_copy(
            src_ref=nb.at[to, pl.ds(2 * j, 2)], dst_ref=rb.at[col, pl.ds(2 * j, 2)],
            send_sem=e_send.at[p, j], recv_sem=e_recv.at[p, j],
            device_id=dev(z, y, to, x), device_id_type=MESH,
        )

    def e_wait(p, j):
        dh, dc = partners[p]
        frm = ((yh * 2 + dh) % 4) + (core + dc) % 2
        pltpu.make_async_remote_copy(
            src_ref=nb.at[frm, pl.ds(2 * j, 2)], dst_ref=rb.at[frm, pl.ds(2 * j, 2)],
            send_sem=e_send.at[p, j], recv_sem=e_recv.at[p, j],
            device_id=dev(z, y, frm, x), device_id_type=MESH,
        ).wait_recv()

    def block(j, h):
        half = (1 - yh) if h == 0 else yh
        base = pl.multiple_of(half * 128, 128)
        total = None
        for xx in range(4):
            w = jnp.concatenate([lt[xx, 2 * j], lt[xx, 2 * j + 1]], axis=1)
            term = jnp.dot(a_b[xx, pl.ds(base, 128), 0:KD], w, preferred_element_type=F32)
            total = term if total is None else total + term
        occ = occ_half[h]
        for g in range(2):
            a = 2 * j + g
            denom = (ene_of(a) + ene_b) - occ
            new = (total[:, g * 128:(g + 1) * 128] / denom).astype(BF16)
            nb[2 * half, a] = new[0:64]
            nb[2 * half + 1, a] = new[64:128]
            of[pl.ds(pl.multiple_of(a * 256 + half * 128, 128), 128), :] = new.astype(F32)
        for p in ((0, 1) if h == 0 else (2,)):
            e_copy(p, j).start()

    def diag_in(j):
        x_fwd(j, 0).wait_recv()
        x_fwd(j, 1).wait_recv()

    def z_copy(p):
        dh, dc = partners[p]
        to = ((yh * 2 + dh) % 4) + (core + dc) % 2
        return pltpu.make_async_remote_copy(
            src_ref=zp.at[to], dst_ref=zr.at[col],
            send_sem=z_send.at[p], recv_sem=z_recv.at[p],
            device_id=dev(z, y, to, x), device_id_type=MESH,
        )

    def z_wait(p):
        dh, dc = partners[p]
        frm = ((yh * 2 + dh) % 4) + (core + dc) % 2
        pltpu.make_async_remote_copy(
            src_ref=zp.at[frm], dst_ref=zr.at[frm],
            send_sem=z_send.at[p], recv_sem=z_recv.at[p],
            device_id=dev(z, y, frm, x), device_id_type=MESH,
        ).wait_recv()

    def cycle(h):
        half = (1 - yh) if h == 0 else yh

        def step(m, acc):
            parts = []
            for u in range(2):
                rows = [of[pl.ds((2 * half + n) * 64 + 2 * m + u, 16, stride=256), :] for n in range(2)]
                parts.append(jnp.concatenate(rows, axis=0).astype(BF16))
            left_op = jnp.concatenate(parts, axis=1)
            return acc + lax.dot_general(left_op, crot[m], (((1,), (1,)), ((), ())), preferred_element_type=F32)

        zsum = lax.fori_loop(0, NK // 2, step, jnp.zeros((32, NQ), F32), unroll=6)
        zw = jnp.concatenate([zsum, jnp.zeros((32, 64), F32)], axis=1)
        for n in range(2):
            zp[2 * half + n] = zw[n * 16:(n + 1) * 16]
        for p in ((0, 1) if h == 0 else (2,)):
            z_copy(p).start()

    diag_in(0)
    block(0, 0)
    forward(3)
    pass_on(1)
    diag_in(1)
    block(1, 0)
    forward(4)
    diag_in(2)
    block(2, 0)
    operand(1)
    block(0, 1)
    diag_in(3)
    block(3, 0)
    block(1, 1)
    block(2, 1)
    diag_in(4)
    block(4, 0)
    cycle(0)
    block(3, 1)
    block(4, 1)
    cycle(1)
    rb[pl.ds(col, 1)] = nb[pl.ds(col, 1)]
    zr[pl.ds(col, 1)] = zp[pl.ds(col, 1)]

    def out_copy(j):
        part = pl.ds(2 * j, 2)
        return pltpu.make_async_copy(out_ref.at[part], out_hbm.at[part], out_sem.at[j])

    z_out = pltpu.make_async_copy(z_ref, z_hbm, out_sem.at[CH])

    lane_o = lax.broadcasted_iota(jnp.int32, (1, 128), 1)
    for j in range(CH):
        for p in range(3):
            e_wait(p, j)
        for h in range(2):
            a = 2 * j + h
            for t in range(3):
                tile = jnp.where(lane_o < 120 - 8 * t, rb[t, a], rb[t + 1, a])
                out_ref[a, :, t * 128:(t + 1) * 128] = tile[:NK]
            out_ref[a, :, 384:480] = rb[3, a][:NK, :96]
        out_copy(j).start()

    for p in range(3):
        z_wait(p)
    zt = (zr[0] + zr[1]) + (zr[2] + zr[3])
    z_ref[:, 0, :] = zt[:NA, :NQ]
    z_out.start()

    for n in range(6):
        @pl.when(jnp.logical_not(s1_here(n)))
        def _():
            s1_copy(n).wait_send()

    @pl.when(relay)
    def _():
        for h in range(2):
            for t in range(1, 4):
                s2_copy(t, h).wait_send()

    for h in range(2):
        for s in range(3):
            sib_copy(s, h).wait_send()

    for j in range(CH):
        for side in range(2):
            x_own(j, side).wait_send()
            x_fwd(j, side).wait_send()
        for p in range(3):
            e_copy(p, j).wait_send()
    for p in range(3):
        z_copy(p).wait_send()
    for j in range(CH):
        out_copy(j).wait()
    z_out.wait()


def hand_on(amps_in, cyc_in, amps_out, cyc_out, amps, cyc, sem_in, sem_out):
    refs = [(amps_in.at[pl.ds(2 * j, 2)], amps.at[pl.ds(2 * j, 2)], amps_out.at[pl.ds(2 * j, 2)]) for j in range(CH)]
    refs.append((cyc_in, cyc, cyc_out))
    reads = [pltpu.make_async_copy(src, mid, sem_in.at[n]) for n, (src, mid, _) in enumerate(refs)]
    writes = [pltpu.make_async_copy(mid, dst, sem_out.at[n]) for n, (_, mid, dst) in enumerate(refs)]
    for copy in reads:
        copy.start()
    for read, write in zip(reads, writes):
        read.wait()
        write.start()
    for copy in writes:
        copy.wait()


def on_device(amp_old, ladder_int, cycle_int, virt_irrep, occ_energy, virt_energy):
    hbm = pl.BlockSpec(memory_space=pltpu.HBM)
    dma = pltpu.SemaphoreType.DMA
    lad = ladder_int.reshape(2 * NA * NB_, ND)
    out_shape = (
        jax.ShapeDtypeStruct((NA, NK, 480), BF16),
        jax.ShapeDtypeStruct((NA, 1, NQ), F32),
    )
    amps, cyc = pl.pallas_call(
        kernel,
        name="ladder",
        out_shape=out_shape,
        in_specs=[hbm] * 6,
        out_specs=(hbm, hbm),
        scratch_shapes=[
            pltpu.VMEM((NA, NK, 480), BF16),
            pltpu.VMEM((NA, 1, NQ), F32),
            pltpu.VMEM((2 * NB_, 256), BF16),
            pltpu.VMEM((20, 2, ND), BF16),
            pltpu.VMEM((2 * NA * NB_, ND), BF16),
            pltpu.VMEM((1, 480), jnp.int32),
            pltpu.VMEM((1, NK), F32),
            pltpu.VMEM((1, 480), F32),
            pltpu.VMEM((8, 512), F32),
            pltpu.VMEM((8, 512), jnp.int32),
            pltpu.VMEM((48, 128), BF16),
            pltpu.VMEM((3, 4, 4, 48, 128), BF16),
            pltpu.VMEM((4, NA, KD, 128), BF16),
            pltpu.VMEM((128, 256), F32),
            pltpu.VMEM((4, 256, 256), BF16),
            pltpu.VMEM((4, NA, 64, 128), BF16),
            pltpu.VMEM((4, NA, 64, 128), BF16),
            pltpu.VMEM((16 * 256, 128), F32),
            pltpu.VMEM((NK, NQ, 480), BF16),
            pltpu.VMEM((NK // 2, NQ, 256), BF16),
            pltpu.VMEM((4, 16, 128), F32),
            pltpu.VMEM((4, 16, 128), F32),
            dma((6,)), dma((6,)), dma, dma((6,)), dma((4, 4)), dma((3, 2)), dma((3, 2)), dma((3, 2)), dma((3, 2)),
            dma((4, CH)), dma((4, CH)), dma((3, CH)), dma((3, CH)), dma((3,)), dma((3,)),
        ],
        compiler_params=pltpu.CompilerParams(
            collective_id=0, has_side_effects=True, vmem_limit_bytes=60 << 20
        ),
    )(
        amp_old, lad, cycle_int,
        virt_irrep.reshape(1, 480), occ_energy.reshape(1, 60), virt_energy.reshape(1, 480),
    )
    amps, cyc = pl.pallas_call(
        hand_on,
        name="hand_on",
        out_shape=out_shape,
        in_specs=[hbm, hbm],
        out_specs=(hbm, hbm),
        scratch_shapes=[
            pltpu.VMEM((NA, NK, 480), BF16),
            pltpu.VMEM((NA, 1, NQ), F32),
            dma((CH + 1,)), dma((CH + 1,)),
        ],
        compiler_params=pltpu.CompilerParams(vmem_limit_bytes=60 << 20),
    )(amps, cyc)
    return amps.transpose(1, 0, 2)[None], cyc.transpose(1, 0, 2)


def solution(mesh):
    placed = (P("row", None, "dep"), P("row", "col", None, "dep"), P(), P(), P(), P())
    return jax.shard_map(
        on_device,
        mesh=mesh,
        in_specs=placed,
        out_specs=(P(("col", "dep"), None, "row", None), P(("col", "dep"), "row", None)),
        check_vma=False,
    )
```

```python
import jax
import jax.numpy as jnp
from jax import lax
from jax.experimental import pallas as pl
from jax.experimental.pallas import tpu as pltpu
from jax.sharding import PartitionSpec as P

MESH = pl.DeviceIdType.MESH
F32 = jnp.float32
BF16 = jnp.bfloat16
NX, NY, NZ = 4, 4, 12
NA, NB_, ND, NK, NQ = 10, 120, 120, 60, 64
CH = 5
KD = 2 * ND


def kernel(
    amp_hbm, lad_hbm, cyc_hbm, irr_hbm, occ_hbm, ene_hbm,
    out_hbm, z_hbm,
    out_ref, z_ref, pick_ref, amp_ref, lad_ref, irr_ref, occ_ref, ene_ref, vec_f, vec_i, shard, sh_all, lt, a_f, a_b, nb, rb, of, cyc, crot, zp, zr,
    in_sem, out_sem, own_sem, s1_send, s1_recv, s2_send, s2_recv, b_send, b_recv, x_send, x_recv, e_send, e_recv, z_send, z_recv,
):
    row = lax.axis_index("row")
    col = lax.axis_index("col")
    x = lax.axis_index("dep")
    z = row // 4
    y = row % 4
    yh = col // 2
    core = col % 2

    def dev(zz, yy, cc, xx):
        return (zz * 4 + yy, cc, xx)

    r12 = 4 * (z % 3) + y
    xt = r12 // 3
    s_mine = r12 % 3
    ip_mine = z // 3
    s_here = (x + y) % 4
    z_off = (3 * x + s_here) // 4
    relay = s_here < 3

    left = (x + 3) % 4
    right = (x + 1) % 4
    diag = (x + 2) % 4

    def pick_matrix():
        sr = lax.broadcasted_iota(jnp.int32, (2 * NB_, 256), 0)
        sc = lax.broadcasted_iota(jnp.int32, (2 * NB_, 256), 1)
        want_b = (sc % 128 + 8 * col) % 128
        return jnp.where(sr == 2 * want_b + sc // 128, 1.0, 0.0).astype(BF16)

    loads = [
        pltpu.make_async_copy(src, dst, in_sem.at[n])
        for n, (src, dst) in enumerate(
            [(amp_hbm, amp_ref), (lad_hbm, lad_ref), (irr_hbm, irr_ref), (occ_hbm, occ_ref), (ene_hbm, ene_ref), (cyc_hbm, cyc)]
        )
    ]
    for copy in loads[:5]:
        copy.start()
    cyc_copy = loads[5]
    barrier = pltpu.get_barrier_semaphore()

    def parity(s):
        return (core + (3 * x + s) // 4 + z) % 2

    def signal(d):
        pl.semaphore_signal(barrier, inc=1, device_id=d, device_id_type=MESH)

    @pl.when(relay)
    def _():
        def go(n, carry):
            zz = 3 * (2 * (n // 4) + parity(s_here)) + z_off
            xx = n % 4

            @pl.when(jnp.logical_or(zz != z, xx != x))
            def _():
                signal(dev(zz, y, col, xx))

            return carry

        lax.fori_loop(0, 8, go, 0)

    for t in range(1, 4):
        signal(dev(z, (y + t) % 4, col, x))
    signal(dev(z, y, col, left))
    signal(dev(z, y, col, right))
    for t in range(1, 4):
        signal(dev(z, y, (col + t) % 4, x))

    pick_ref[...] = pick_matrix()
    loads[0].wait()

    raw = amp_ref[...]
    wide = jnp.concatenate(
        [raw[:, 0, :].astype(F32), raw[:, 1, :].astype(F32), jnp.zeros((20, 16), F32)], axis=1
    )
    gap = jnp.zeros((4, 128), F32)
    shard[...] = jnp.concatenate([wide[:, :128], gap, wide[:, 128:], gap], axis=0).astype(BF16)

    pl.semaphore_wait(barrier, 8 + 6 - jnp.where(jnp.logical_and(xt == x, core == 0), 1, 0))

    def s1_plane(n):
        even = (6, 8, 4, 10, 2, 0)[n]
        odd = (5, 7, 3, 9, 1, 11)[n]
        return (z + jnp.where(core == 0, even, odd)) % 12

    def s1_copy(n):
        zz = s1_plane(n)
        return pltpu.make_async_remote_copy(
            src_ref=shard, dst_ref=sh_all.at[s_mine, ip_mine, x],
            send_sem=s1_send.at[n], recv_sem=s1_recv.at[ip_mine, x],
            device_id=dev(zz, y, col, xt), device_id_type=MESH,
        )

    def s1_here(n):
        return jnp.logical_and(s1_plane(n) == z, xt == x)

    stays = jnp.logical_and(xt == x, core == 0)

    def s1_go(n, carry):
        @pl.when(jnp.logical_not(s1_here(n)))
        def _():
            s1_copy(n).start()

        return carry

    for n in range(6):
        s1_go(n, 0)

    @pl.when(stays)
    def _():
        pltpu.make_async_copy(shard, sh_all.at[s_mine, ip_mine, x], own_sem).start()

    for copy in loads[2:5]:
        copy.wait()

    vec_f[...] = jnp.zeros_like(vec_f)
    vec_i[...] = jnp.zeros_like(vec_i)
    vec_f[0:1, 0:480] = ene_ref[...]
    vec_f[1:2, 0:60] = occ_ref[...]
    vec_i[0:1, 0:480] = irr_ref[...]
    lane = lax.broadcasted_iota(jnp.int32, (1, 128), 1)
    edge = 120 - 8 * col
    prev = jnp.maximum(col - 1, 0)
    at = pl.multiple_of(col * 128, 128)
    before = pl.multiple_of(prev * 128, 128)
    ene_b = jnp.where(lane < edge, vec_f[0:1, pl.ds(at, 128)], vec_f[0:1, pl.ds(before, 128)])
    irr_b = jnp.where(lane < edge, vec_i[0:1, pl.ds(at, 128)], vec_i[0:1, pl.ds(before, 128)])
    ii = lax.broadcasted_iota(jnp.int32, (ND, 512), 0)
    jj = lax.broadcasted_iota(jnp.int32, (ND, 512), 1)
    irr_d = jnp.sum(jnp.where(jj == ii + ND * x, vec_i[0:1, :].astype(F32), 0.0), axis=1, keepdims=True).astype(jnp.int32)
    wide_lane = lax.broadcasted_iota(jnp.int32, (1, 512), 1)

    def ene_of(a):
        return jnp.sum(jnp.where(wide_lane == row * NA + a, vec_f[0:1, :], 0.0), axis=1, keepdims=True)

    def irr_of(n):
        picked = jnp.sum(jnp.where(wide_lane == n, vec_i[0:1, :].astype(F32), 0.0), axis=1, keepdims=True)
        return picked.astype(jnp.int32)

    irr_c = [irr_of(c) for c in range(2)]

    def prep(a, carry):
        block = lad_ref[pl.ds(pl.multiple_of(a * 240, 240), 240), :]
        got = lax.dot_general(block, pick_ref[...], (((0,), (0,)), ((), ())), preferred_element_type=F32)
        ab = jnp.bitwise_xor(irr_b, irr_of(row * NA + a))
        both = []
        for c in range(2):
            keep = jnp.bitwise_xor(ab, irr_c[c]) == irr_d
            both.append(jnp.where(keep, got[:, c * 128:(c + 1) * 128], 0.0))
        lt[x, a] = jnp.concatenate(both, axis=0).astype(BF16)
        return carry

    def x_own(j, side):
        return pltpu.make_async_remote_copy(
            src_ref=lt.at[x, pl.ds(2 * j, 2)], dst_ref=lt.at[x, pl.ds(2 * j, 2)],
            send_sem=x_send.at[side, j], recv_sem=x_recv.at[side, j],
            device_id=dev(z, y, col, left if side == 0 else right), device_id_type=MESH,
        )

    def x_fwd(j, side):
        owner = right if side == 0 else left
        a = 2 * j + (1 if side == 0 else 0)
        return pltpu.make_async_remote_copy(
            src_ref=lt.at[owner, a], dst_ref=lt.at[owner, a],
            send_sem=x_send.at[2 + side, j], recv_sem=x_recv.at[2 + side, j],
            device_id=dev(z, y, col, left if side == 0 else right), device_id_type=MESH,
        )

    cyc_copy.start()
    loads[1].wait()
    for j in range(CH):
        lax.fori_loop(2 * j, 2 * j + 2, prep, 0)
        if j < 3:
            x_own(j, 0).start()
            x_own(j, 1).start()

    a_f[...] = jnp.zeros_like(a_f)
    of[NA * 256:, :] = jnp.zeros((6 * 256, 128), F32)
    pi = lax.broadcasted_iota(jnp.int32, (128, 128), 0)
    pj = lax.broadcasted_iota(jnp.int32, (128, 128), 1)
    occ_row = vec_f[1:2, 0:128]
    def occ_i_of(half):
        return jnp.sum(jnp.where(pj == (2 * half + pi // 64) * 4 + x, occ_row, 0.0), axis=1, keepdims=True)

    occ_k = jnp.sum(jnp.where(pj == pi % 64, occ_row, 0.0), axis=1, keepdims=True)
    occ_half = [occ_i_of(1 - yh) + occ_k, occ_i_of(yh) + occ_k]


    cyc_copy.wait()
    lane3 = lax.broadcasted_iota(jnp.int32, (1, 1, 128), 2)
    for t in range(4):
        @pl.when(col == t)
        def _():
            def rot(m, carry):
                lo = max(t - 1, 0) * 128
                for u in range(2):
                    k = 2 * m + u
                    if t < 3:
                        here = cyc[pl.ds(k, 1), :, t * 128:(t + 1) * 128]
                    else:
                        here = jnp.concatenate(
                            [cyc[pl.ds(k, 1), :, 384:480], cyc[pl.ds(k, 1), :, 352:384]], axis=2
                        )
                    there = cyc[pl.ds(k, 1), :, lo:lo + 128]
                    crot[pl.ds(m, 1), :, u * 128:(u + 1) * 128] = jnp.where(lane3 < 120 - 8 * t, here, there)
                return carry

            lax.fori_loop(0, NK // 2, rot, 0)

    def unit(s, h, mine):
        half = (1 - yh) if h == 0 else yh
        share = parity(s) if mine else 1 - parity(s)
        return sh_all.at[s, 2 * half + share]

    def s2_copy(t, h):
        return pltpu.make_async_remote_copy(
            src_ref=unit(s_here, h, True), dst_ref=unit(s_here, h, True),
            send_sem=s2_send.at[t - 1, h], recv_sem=s2_recv.at[s_here, h],
            device_id=dev(z, (y + t) % 4, col, x), device_id_type=MESH,
        )

    def s2_wait(s, h):
        return pltpu.make_async_remote_copy(
            src_ref=unit(s, h, True), dst_ref=unit(s, h, True),
            send_sem=s2_send.at[0, h], recv_sem=s2_recv.at[s, h],
            device_id=dev(z, (y + 1) % 4, col, x), device_id_type=MESH,
        )

    other = 2 * yh + 1 - core

    def sib_copy(s, h):
        return pltpu.make_async_remote_copy(
            src_ref=unit(s, h, True), dst_ref=unit(s, h, True),
            send_sem=b_send.at[s, h], recv_sem=b_recv.at[s, h],
            device_id=dev(z, y, other, x), device_id_type=MESH,
        )

    def sib_wait(s, h):
        return pltpu.make_async_remote_copy(
            src_ref=unit(s, h, False), dst_ref=unit(s, h, False),
            send_sem=b_send.at[s, h], recv_sem=b_recv.at[s, h],
            device_id=dev(z, y, other, x), device_id_type=MESH,
        )

    def forward(j):
        x_own(j, 0).wait_recv()
        x_own(j, 1).wait_recv()
        x_fwd(j, 0).start()
        x_fwd(j, 1).start()
        if j + 3 < CH:
            x_own(j + 3, 0).start()
            x_own(j + 3, 1).start()

    forward(0)

    @pl.when(stays)
    def _():
        pltpu.make_async_copy(shard, sh_all.at[s_mine, ip_mine, x], own_sem).wait()

    @pl.when(relay)
    def _():
        for h in range(2):
            half = (1 - yh) if h == 0 else yh
            i4 = 2 * half + parity(s_here)
            zz = 3 * i4 + z_off

            def got(xx, carry):
                @pl.when(jnp.logical_or(zz != z, xx != x))
                def _():
                    pltpu.make_async_remote_copy(
                        src_ref=shard, dst_ref=sh_all.at[s_here, i4, xx],
                        send_sem=s1_send.at[0], recv_sem=s1_recv.at[i4, xx],
                        device_id=dev(z, y, other, x), device_id_type=MESH,
                    ).wait_recv()

                return carry

            lax.fori_loop(0, 4, got, 0)
            for t in (2, 1, 3):
                s2_copy(t, h).start()
            sib_copy(s_here, h).start()

    def pass_on(h):
        for s in range(3):
            @pl.when(s_here != s)
            def _():
                s2_wait(s, h).wait_recv()
                sib_copy(s, h).start()

    def operand(h):
        half = (1 - yh) if h == 0 else yh
        for s in range(3):
            sib_wait(s, h).wait_recv()
        base = pl.multiple_of(half * 128, 128)
        for xx in range(4):
            for n in range(2):
                for s in range(3):
                    got = sh_all[s, 2 * half + n, xx].astype(F32)
                    top = n * 64 + s * 20
                    a_f[top:top + 20, 0:128] = got[0:20]
                    a_f[top:top + 20, 128:256] = got[24:44]
            a_b[xx, pl.ds(base, 128), :] = a_f[...].astype(BF16)

    forward(1)
    forward(2)
    pass_on(0)
    operand(0)

    partners = [(2, 0), (2, 1), (0, 1)]

    def e_copy(p, j):
        dh, dc = partners[p]
        to = ((yh * 2 + dh) % 4) + (core + dc) % 2
        return pltpu.make_async_remote_copy(
            src_ref=nb.at[to, pl.ds(2 * j, 2)], dst_ref=rb.at[col, pl.ds(2 * j, 2)],
            send_sem=e_send.at[p, j], recv_sem=e_recv.at[p, j],
            device_id=dev(z, y, to, x), device_id_type=MESH,
        )

    def e_wait(p, j):
        dh, dc = partners[p]
        frm = ((yh * 2 + dh) % 4) + (core + dc) % 2
        pltpu.make_async_remote_copy(
            src_ref=nb.at[frm, pl.ds(2 * j, 2)], dst_ref=rb.at[frm, pl.ds(2 * j, 2)],
            send_sem=e_send.at[p, j], recv_sem=e_recv.at[p, j],
            device_id=dev(z, y, frm, x), device_id_type=MESH,
        ).wait_recv()

    def block(j, h):
        half = (1 - yh) if h == 0 else yh
        base = pl.multiple_of(half * 128, 128)
        total = None
        for xx in range(4):
            w = jnp.concatenate([lt[xx, 2 * j], lt[xx, 2 * j + 1]], axis=1)
            term = jnp.dot(a_b[xx, pl.ds(base, 128), 0:KD], w, preferred_element_type=F32)
            total = term if total is None else total + term
        occ = occ_half[h]
        for g in range(2):
            a = 2 * j + g
            denom = (ene_of(a) + ene_b) - occ
            new = (total[:, g * 128:(g + 1) * 128] / denom).astype(BF16)
            nb[2 * half, a] = new[0:64]
            nb[2 * half + 1, a] = new[64:128]
            of[pl.ds(pl.multiple_of(a * 256 + half * 128, 128), 128), :] = new.astype(F32)
        for p in ((0, 1) if h == 0 else (2,)):
            e_copy(p, j).start()

    def diag_in(j):
        x_fwd(j, 0).wait_recv()
        x_fwd(j, 1).wait_recv()

    def z_copy(p):
        dh, dc = partners[p]
        to = ((yh * 2 + dh) % 4) + (core + dc) % 2
        return pltpu.make_async_remote_copy(
            src_ref=zp.at[to], dst_ref=zr.at[col],
            send_sem=z_send.at[p], recv_sem=z_recv.at[p],
            device_id=dev(z, y, to, x), device_id_type=MESH,
        )

    def z_wait(p):
        dh, dc = partners[p]
        frm = ((yh * 2 + dh) % 4) + (core + dc) % 2
        pltpu.make_async_remote_copy(
            src_ref=zp.at[frm], dst_ref=zr.at[frm],
            send_sem=z_send.at[p], recv_sem=z_recv.at[p],
            device_id=dev(z, y, frm, x), device_id_type=MESH,
        ).wait_recv()

    def cycle(h):
        half = (1 - yh) if h == 0 else yh

        def step(m, acc):
            parts = []
            for u in range(2):
                rows = [of[pl.ds((2 * half + n) * 64 + 2 * m + u, 16, stride=256), :] for n in range(2)]
                parts.append(jnp.concatenate(rows, axis=0).astype(BF16))
            left_op = jnp.concatenate(parts, axis=1)
            return acc + lax.dot_general(left_op, crot[m], (((1,), (1,)), ((), ())), preferred_element_type=F32)

        zsum = lax.fori_loop(0, NK // 2, step, jnp.zeros((32, NQ), F32), unroll=6)
        zw = jnp.concatenate([zsum, jnp.zeros((32, 64), F32)], axis=1)
        for n in range(2):
            zp[2 * half + n] = zw[n * 16:(n + 1) * 16]
        for p in ((0, 1) if h == 0 else (2,)):
            z_copy(p).start()

    diag_in(0)
    block(0, 0)
    forward(3)
    pass_on(1)
    diag_in(1)
    block(1, 0)
    forward(4)
    diag_in(2)
    block(2, 0)
    diag_in(3)
    block(3, 0)
    operand(1)
    block(0, 1)
    block(1, 1)
    block(2, 1)
    diag_in(4)
    block(4, 0)
    cycle(0)
    block(3, 1)
    block(4, 1)
    cycle(1)
    rb[pl.ds(col, 1)] = nb[pl.ds(col, 1)]
    zr[pl.ds(col, 1)] = zp[pl.ds(col, 1)]

    def out_copy(j):
        part = pl.ds(2 * j, 2)
        return pltpu.make_async_copy(out_ref.at[part], out_hbm.at[part], out_sem.at[j])

    z_out = pltpu.make_async_copy(z_ref, z_hbm, out_sem.at[CH])

    lane_o = lax.broadcasted_iota(jnp.int32, (1, 128), 1)
    for j in range(CH):
        for p in range(3):
            e_wait(p, j)
        for h in range(2):
            a = 2 * j + h
            for t in range(3):
                tile = jnp.where(lane_o < 120 - 8 * t, rb[t, a], rb[t + 1, a])
                out_ref[a, :, t * 128:(t + 1) * 128] = tile[:NK]
            out_ref[a, :, 384:480] = rb[3, a][:NK, :96]
        out_copy(j).start()

    for p in range(3):
        z_wait(p)
    zt = (zr[0] + zr[1]) + (zr[2] + zr[3])
    z_ref[:, 0, :] = zt[:NA, :NQ]
    z_out.start()

    for n in range(6):
        @pl.when(jnp.logical_not(s1_here(n)))
        def _():
            s1_copy(n).wait_send()

    @pl.when(relay)
    def _():
        for h in range(2):
            for t in range(1, 4):
                s2_copy(t, h).wait_send()

    for h in range(2):
        for s in range(3):
            sib_copy(s, h).wait_send()

    for j in range(CH):
        for side in range(2):
            x_own(j, side).wait_send()
            x_fwd(j, side).wait_send()
        for p in range(3):
            e_copy(p, j).wait_send()
    for p in range(3):
        z_copy(p).wait_send()
    for j in range(CH):
        out_copy(j).wait()
    z_out.wait()


def hand_on(amps_in, cyc_in, amps_out, cyc_out, amps, cyc, sem_in, sem_out):
    refs = [(amps_in.at[pl.ds(2 * j, 2)], amps.at[pl.ds(2 * j, 2)], amps_out.at[pl.ds(2 * j, 2)]) for j in range(CH)]
    refs.append((cyc_in, cyc, cyc_out))
    reads = [pltpu.make_async_copy(src, mid, sem_in.at[n]) for n, (src, mid, _) in enumerate(refs)]
    writes = [pltpu.make_async_copy(mid, dst, sem_out.at[n]) for n, (_, mid, dst) in enumerate(refs)]
    for copy in reads:
        copy.start()
    for read, write in zip(reads, writes):
        read.wait()
        write.start()
    for copy in writes:
        copy.wait()


def on_device(amp_old, ladder_int, cycle_int, virt_irrep, occ_energy, virt_energy):
    hbm = pl.BlockSpec(memory_space=pltpu.HBM)
    dma = pltpu.SemaphoreType.DMA
    lad = ladder_int.reshape(2 * NA * NB_, ND)
    out_shape = (
        jax.ShapeDtypeStruct((NA, NK, 480), BF16),
        jax.ShapeDtypeStruct((NA, 1, NQ), F32),
    )
    amps, cyc = pl.pallas_call(
        kernel,
        name="ladder",
        out_shape=out_shape,
        in_specs=[hbm] * 6,
        out_specs=(hbm, hbm),
        scratch_shapes=[
            pltpu.VMEM((NA, NK, 480), BF16),
            pltpu.VMEM((NA, 1, NQ), F32),
            pltpu.VMEM((2 * NB_, 256), BF16),
            pltpu.VMEM((20, 2, ND), BF16),
            pltpu.VMEM((2 * NA * NB_, ND), BF16),
            pltpu.VMEM((1, 480), jnp.int32),
            pltpu.VMEM((1, NK), F32),
            pltpu.VMEM((1, 480), F32),
            pltpu.VMEM((8, 512), F32),
            pltpu.VMEM((8, 512), jnp.int32),
            pltpu.VMEM((48, 128), BF16),
            pltpu.VMEM((3, 4, 4, 48, 128), BF16),
            pltpu.VMEM((4, NA, KD, 128), BF16),
            pltpu.VMEM((128, 256), F32),
            pltpu.VMEM((4, 256, 256), BF16),
            pltpu.VMEM((4, NA, 64, 128), BF16),
            pltpu.VMEM((4, NA, 64, 128), BF16),
            pltpu.VMEM((16 * 256, 128), F32),
            pltpu.VMEM((NK, NQ, 480), BF16),
            pltpu.VMEM((NK // 2, NQ, 256), BF16),
            pltpu.VMEM((4, 16, 128), F32),
            pltpu.VMEM((4, 16, 128), F32),
            dma((6,)), dma((6,)), dma, dma((6,)), dma((4, 4)), dma((3, 2)), dma((3, 2)), dma((3, 2)), dma((3, 2)),
            dma((4, CH)), dma((4, CH)), dma((3, CH)), dma((3, CH)), dma((3,)), dma((3,)),
        ],
        compiler_params=pltpu.CompilerParams(
            collective_id=0, has_side_effects=True, vmem_limit_bytes=60 << 20
        ),
    )(
        amp_old, lad, cycle_int,
        virt_irrep.reshape(1, 480), occ_energy.reshape(1, 60), virt_energy.reshape(1, 480),
    )
    amps, cyc = pl.pallas_call(
        hand_on,
        name="hand_on",
        out_shape=out_shape,
        in_specs=[hbm, hbm],
        out_specs=(hbm, hbm),
        scratch_shapes=[
            pltpu.VMEM((NA, NK, 480), BF16),
            pltpu.VMEM((NA, 1, NQ), F32),
            dma((CH + 1,)), dma((CH + 1,)),
        ],
        compiler_params=pltpu.CompilerParams(vmem_limit_bytes=60 << 20),
    )(amps, cyc)
    return amps.transpose(1, 0, 2)[None], cyc.transpose(1, 0, 2)


def solution(mesh):
    placed = (P("row", None, "dep"), P("row", "col", None, "dep"), P(), P(), P(), P())
    return jax.shard_map(
        on_device,
        mesh=mesh,
        in_specs=placed,
        out_specs=(P(("col", "dep"), None, "row", None), P(("col", "dep"), "row", None)),
        check_vma=False,
    )
```
